128 devices in a mesh: seq: 16 (over x_lo, y, core), head: 8 (over z, x_hi).
Axes of the slice: x: 4 (x_hi: 2, x_lo: 2; x = x_hi * 2 + x_lo), y: 4, z: 4, core: 2. Of those that a mesh axis runs over, the one named last changes fastest.
Arguments:
- out_grad: bfloat16 [16384, 6144], P(('seq', 'head')), may hold values from -96 to 96
- expert_rows: bfloat16 [8, 8192, 6144], P('head', 'seq'), may hold values from -96 to 96
- expert_ids: int32 [16384, 2], P(('seq', 'head')), may hold values from 0 to 7, all different within a row; in each aligned block of 128 rows (0 to 127, 128 to 255, ...) at most 64 rows name the same one
- gates: float32 [16384, 2], P(('seq', 'head')), may hold values from 0.1 to 0.9
- out_proj: bfloat16 [3072, 6144], P('head'), may hold values from -0.078125 to 0.078125
- attention_output: bfloat16 [24, 16384, 128], P('head', 'seq'), may hold values from -0.0029296875 to 0.0029296875
- saved_queries: bfloat16 [24, 16384, 128], P('head', 'seq'), may hold values from -1.6953125 to 1.6953125
- saved_keys: bfloat16 [8, 16384, 128], P('head', 'seq'), may hold values from -1.6953125 to 1.6953125
- saved_values: bfloat16 [8, 16384, 128], P('head', 'seq'), may hold values from -6 to 6
- softmax_normalizer: float32 [24, 16384], P('head', 'seq'), may hold values from 8 to 9.5
Outputs:
- grad_query: bfloat16 [16384, 3072], P(('seq', 'head'))
- key_gradient_rows: bfloat16 [16384, 1024], P(('seq', 'head'))
- value_gradient_rows: bfloat16 [16384, 1024], P(('seq', 'head'))
- grad_proj: bfloat16 [3072, 6144], P('head')
The draws below stay inside these ranges and needn't reach their ends.
Inputs may be any that keep to these rules, and one draw needn't show every extreme that they name: `expert_ids`: each row names 2 different experts. In each aligned block of 128 rows (the tokens of one device) no expert is named more than 64 times, a bound that some block reaches.
All inputs are finite; a program needn't handle non-finite values.
Results may differ from the reference program's by a relative error of at most 0.0065.
Values may be sent and summed in bfloat16 or wider, within the bound.
A program may use at most 128 MiB of HBM per device.

```python
import math
import jax
import jax.numpy as jnp
import numpy as np
from jax import lax

D = 6144
HEAD_SIZE = 128
KEY_VALUE_HEADS = 8
QUERY_PER_KV = 3
EXPERTS = 8
TOP = 2
WIN = 4096
SEQ_DEV = 1024
SEQUENCE_TOKENS = 16384
TOK_DEV = 128
CAP = 64
HQ = 24
SLOTS = 8192
N_SEQ = 16
N_HEAD = 8


def block_scale(own_key, dims, cuts, least, largest):
    def one(dim, shards_of):
        draws = jax.random.uniform(jax.random.fold_in(jax.random.fold_in(own_key, 6), dim), (shards_of,), jnp.float32, least / len(cuts), largest / len(cuts))
        return jnp.repeat(jnp.exp(draws), dims[dim] // shards_of).reshape((-1,) + (1,) * (len(dims) - dim - 1))

    gain = one(*cuts[0])
    for cut in cuts[1:]:
        gain = gain * one(*cut)
    return gain


def routed_block(stream_key, own, number, rows, count, top, limit, lean):
    ranking = jax.random.permutation(stream_key, count)
    packed, common = shares(count, rows * top, limit, lean, True), shares(count, rows * top, limit, lean, False)
    places = jnp.arange(count)

    def named(lengths, turn):
        used = int((lengths > 0).sum())
        fixed = max(1, used // 4)
        passed = fixed + (places - fixed + turn * (used - fixed)) % max(1, count - fixed)
        return jnp.zeros((count,), jnp.int32).at[ranking[jnp.where(places < fixed, places, passed)]].set(jnp.asarray(lengths, jnp.int32))

    lengths = jnp.where(number % 4 == 0, named(packed, number // 4), named(common, number - number // 4 - 1))
    mixed = jax.random.permutation(jax.random.fold_in(own, 3), count)
    donor, sink = mixed[0:count // 2 * 2:2], mixed[1:count // 2 * 2:2]
    slack = jnp.minimum(lengths[donor] - 1, limit - lengths[sink]) // 2
    slack = jnp.where((donor == ranking[0]) | (sink == ranking[0]) | (lengths[sink] == 0), 0, jnp.maximum(slack, 0))
    passed = jax.random.randint(jax.random.fold_in(own, 4), (count // 2,), 0, 1 << 20) % (slack + 1)
    lengths = lengths.at[donor].add(-passed).at[sink].add(passed)
    items = jnp.searchsorted(jnp.cumsum(lengths), jnp.arange(rows * top), side="right").astype(jnp.int32)
    grid = items.reshape(top, rows).T
    grid = grid[jax.random.permutation(jax.random.fold_in(own, 1), rows)]
    turn = jax.random.randint(jax.random.fold_in(own, 2), (rows, 1), 0, top)
    return jnp.take_along_axis(grid, (jnp.arange(top)[None, :] + turn) % top, axis=1)


def shares(number_of, total, limit, slope, full):
    loads = [(1 << 20) // math.isqrt(grade ** slope) + 1 for grade in range(1, number_of + 1)]
    largest = limit if full else min(limit, max(-(-total // number_of), total * loads[0] // sum(loads)))
    least = 1 if total - largest >= number_of - 1 else 0
    counts, rest = [largest] + [least] * (number_of - 1), total - largest - least * (number_of - 1)
    while rest > 0:
        candidates = [i for i in range(1, number_of) if counts[i] < largest] or [i for i in range(1, number_of) if counts[i] < limit]
        whole, budget = sum([loads[i] for i in candidates]), rest
        for i in candidates:
            addition = min(limit - counts[i], max(1, budget * loads[i] // whole), rest)
            counts[i] = counts[i] + addition
            rest = rest - addition
    return np.array(counts)


def bell_draw(rng, extent, spread, limit, cuts=(), held_as=jnp.bfloat16):
    entries = jax.random.normal(rng, extent, jnp.float32) * spread
    if len(cuts) > 0:
        entries = block_scale(rng, extent, cuts, -0.22, 0.18) * entries
    return jnp.clip(entries, min=-limit, max=limit).astype(held_as)


def setup_inputs(seed: int = 0) -> dict:
    seeds = jax.random.split(jax.random.key(seed), 11)
    out_grad = bell_draw(seeds[0], (SEQUENCE_TOKENS, D), 16.0, 96.0, ((0, 128),))
    expert_rows = bell_draw(seeds[1], (EXPERTS, SLOTS, D), 16.0, 96.0, ((0, 8), (1, 16)))
    expert_ids_keys = jax.random.split(jax.random.fold_in(seeds[2], 1), SEQUENCE_TOKENS // TOK_DEV)
    expert_ids_turns = jax.random.permutation(jax.random.fold_in(seeds[2], 3), SEQUENCE_TOKENS // TOK_DEV)
    expert_ids = jax.vmap(lambda own, number: routed_block(jax.random.fold_in(seeds[2], 2), own, number, TOK_DEV, EXPERTS, TOP, CAP, 2))(expert_ids_keys, expert_ids_turns).reshape((SEQUENCE_TOKENS, TOP))
    gates = jnp.clip(0.1 + 0.79999997 * jax.random.uniform(seeds[3], (SEQUENCE_TOKENS, TOP), jnp.float32) ** block_scale(seeds[3], (SEQUENCE_TOKENS, TOP), ((0, 128),), -0.2, 0.2), 0.1, 0.9)
    out_proj = bell_draw(seeds[4], (HQ * HEAD_SIZE, D), D ** -0.5, 0.078125, ((0, 8),))
    attention_output = bell_draw(seeds[5], (HQ, SEQUENCE_TOKENS, HEAD_SIZE), 0.00048828125, 0.0029296875, ((0, 8), (1, 16)))
    saved_queries = jnp.clip(jax.random.uniform(seeds[6], (HQ, SEQUENCE_TOKENS, HEAD_SIZE), jnp.float32, -1.6953125, 1.6953125) * block_scale(seeds[6], (HQ, SEQUENCE_TOKENS, HEAD_SIZE), ((0, 8), (1, 16)), -0.4, 0.0), -1.6953125, 1.6953125).astype(jnp.bfloat16)
    saved_keys = jnp.clip(jax.random.uniform(seeds[7], (KEY_VALUE_HEADS, SEQUENCE_TOKENS, HEAD_SIZE), jnp.float32, -1.6953125, 1.6953125) * block_scale(seeds[7], (KEY_VALUE_HEADS, SEQUENCE_TOKENS, HEAD_SIZE), ((0, 8), (1, 16)), -0.4, 0.0), -1.6953125, 1.6953125).astype(jnp.bfloat16)
    saved_values = bell_draw(seeds[8], (KEY_VALUE_HEADS, SEQUENCE_TOKENS, HEAD_SIZE), 1.0, 6.0, ((0, 8), (1, 16)))
    softmax_normalizer = jnp.clip(8.0 + 1.5 * jax.random.uniform(seeds[9], (HQ, SEQUENCE_TOKENS), jnp.float32) ** block_scale(seeds[9], (HQ, SEQUENCE_TOKENS), ((0, 8), (1, 16)), -0.2, 0.2), 8.0, 9.5)
    return dict(out_grad=out_grad, expert_rows=expert_rows, expert_ids=expert_ids, gates=gates, out_proj=out_proj, attention_output=attention_output, saved_queries=saved_queries, saved_keys=saved_keys, saved_values=saved_values, softmax_normalizer=softmax_normalizer)


def combine_rows(out_grad, expert_rows, expert_ids, gates):
    devices = N_SEQ * N_HEAD
    pair_ids = expert_ids.reshape(devices, TOK_DEV * TOP)
    onehot = (pair_ids[:, :, None] == jnp.arange(EXPERTS, dtype=jnp.int32)[None, None, :]).astype(jnp.int32)
    before = jnp.cumsum(onehot, axis=1) - onehot
    slot_rank = lax.optimization_barrier(jnp.sum(before * onehot, axis=2))
    source = jnp.arange(devices, dtype=jnp.int32)[:, None]
    slot_index = (source * CAP + slot_rank).astype(jnp.int32)
    picked = expert_rows[pair_ids, slot_index].reshape(SEQUENCE_TOKENS, TOP, D)
    summed = out_grad.astype(jnp.float32)
    summed = summed + gates[:, 0:1] * picked[:, 0].astype(jnp.float32)
    summed = summed + gates[:, 1:2] * picked[:, 1].astype(jnp.float32)
    return summed.astype(jnp.bfloat16)

def band_grads(input_arrays):
    q_group, key_rows, value_rows, grad_group, out_group, lse_group = input_arrays
    block_rows = min(512, SEQ_DEV)
    key_span = WIN + block_rows
    score_scale = 1.0 / math.sqrt(HEAD_SIZE)
    key_pad = jnp.concatenate([jnp.zeros((WIN, HEAD_SIZE), key_rows.dtype), key_rows], axis=0)
    value_pad = jnp.concatenate([jnp.zeros((WIN, HEAD_SIZE), value_rows.dtype), value_rows], axis=0)
    row_delta = lax.optimization_barrier(jnp.sum(grad_group.astype(jnp.float32) * out_group.astype(jnp.float32), axis=2))
    rows_iota = lax.broadcasted_iota(jnp.int32, (block_rows, key_span), 0)
    cols_iota = lax.broadcasted_iota(jnp.int32, (block_rows, key_span), 1)
    in_band = (cols_iota >= rows_iota + 1) & (cols_iota <= rows_iota + WIN)

    def scan_step(carry, index):
        key_grad, value_grad = carry
        first_row = (index * block_rows).astype(jnp.int32)
        usable = in_band & (cols_iota + first_row >= WIN)
        key_blk = lax.dynamic_slice_in_dim(key_pad, first_row, key_span, 0)
        value_blk = lax.dynamic_slice_in_dim(value_pad, first_row, key_span, 0)
        dk_blk = jnp.zeros((key_span, HEAD_SIZE), jnp.float32)
        dv_blk = jnp.zeros((key_span, HEAD_SIZE), jnp.float32)
        dq_rows = []
        for q_head in range(QUERY_PER_KV):
            query_blk = lax.dynamic_slice_in_dim(q_group[q_head], first_row, block_rows, 0)
            grad_blk = lax.dynamic_slice_in_dim(grad_group[q_head], first_row, block_rows, 0)
            lse_blk = lax.dynamic_slice_in_dim(lse_group[q_head], first_row, block_rows, 0)
            delta_blk = lax.dynamic_slice_in_dim(row_delta[q_head], first_row, block_rows, 0)
            scores = jnp.dot(query_blk, key_blk.T, preferred_element_type=jnp.float32) * score_scale
            probability = jnp.where(usable, jnp.exp(scores - lse_blk[:, None]), 0.0)
            grad_prob = jnp.dot(grad_blk, value_blk.T, preferred_element_type=jnp.float32)
            grad_score = probability * (grad_prob - delta_blk[:, None])
            prob_half = probability.astype(jnp.bfloat16)
            score_half = grad_score.astype(jnp.bfloat16)
            dv_blk = dv_blk + jnp.dot(prob_half.T, grad_blk, preferred_element_type=jnp.float32)
            dk_blk = dk_blk + score_scale * jnp.dot(score_half.T, query_blk, preferred_element_type=jnp.float32)
            dq_rows.append(score_scale * jnp.dot(score_half, key_blk, preferred_element_type=jnp.float32))
        old_key = lax.dynamic_slice_in_dim(key_grad, first_row, key_span, 0)
        key_grad = lax.dynamic_update_slice_in_dim(key_grad, old_key + dk_blk, first_row, 0)
        old_value = lax.dynamic_slice_in_dim(value_grad, first_row, key_span, 0)
        value_grad = lax.dynamic_update_slice_in_dim(value_grad, old_value + dv_blk, first_row, 0)
        return ((key_grad, value_grad), jnp.stack(dq_rows, axis=0))
    start_carry = (jnp.zeros((WIN + SEQUENCE_TOKENS, HEAD_SIZE), jnp.float32), jnp.zeros((WIN + SEQUENCE_TOKENS, HEAD_SIZE), jnp.float32))
    (key_grad, value_grad), dq_blocks = lax.scan(scan_step, start_carry, jnp.arange(SEQUENCE_TOKENS // block_rows, dtype=jnp.int32))
    dq_full = jnp.transpose(dq_blocks, (1, 0, 2, 3)).reshape(QUERY_PER_KV, SEQUENCE_TOKENS, HEAD_SIZE)
    return (dq_full, key_grad[WIN:], value_grad[WIN:])

def reference(out_grad, expert_rows, expert_ids, gates, out_proj, attention_output, saved_queries, saved_keys, saved_values, softmax_normalizer):
    hidden = combine_rows(out_grad, expert_rows, expert_ids, gates)
    grad_out = jnp.dot(hidden, out_proj.T, preferred_element_type=jnp.float32).astype(jnp.bfloat16)
    out_mat = jnp.transpose(attention_output, (1, 0, 2)).reshape(SEQUENCE_TOKENS, HQ * HEAD_SIZE)
    grad_proj = jnp.dot(out_mat.T, hidden, preferred_element_type=jnp.float32).astype(jnp.bfloat16)
    head_gradients = jnp.transpose(grad_out.reshape(SEQUENCE_TOKENS, HQ, HEAD_SIZE), (1, 0, 2))
    input_arrays = (saved_queries.reshape(KEY_VALUE_HEADS, QUERY_PER_KV, SEQUENCE_TOKENS, HEAD_SIZE), saved_keys, saved_values, head_gradients.reshape(KEY_VALUE_HEADS, QUERY_PER_KV, SEQUENCE_TOKENS, HEAD_SIZE), attention_output.reshape(KEY_VALUE_HEADS, QUERY_PER_KV, SEQUENCE_TOKENS, HEAD_SIZE), softmax_normalizer.reshape(KEY_VALUE_HEADS, QUERY_PER_KV, SEQUENCE_TOKENS))
    dq_all, key_gradient_full, value_gradient_full = lax.map(band_grads, input_arrays)
    grad_query = jnp.transpose(dq_all.reshape(HQ, SEQUENCE_TOKENS, HEAD_SIZE), (1, 0, 2)).reshape(SEQUENCE_TOKENS, HQ * HEAD_SIZE).astype(jnp.bfloat16)
    key_gradient_rows = jnp.transpose(key_gradient_full, (1, 0, 2)).reshape(SEQUENCE_TOKENS, KEY_VALUE_HEADS * HEAD_SIZE).astype(jnp.bfloat16)
    value_gradient_rows = jnp.transpose(value_gradient_full, (1, 0, 2)).reshape(SEQUENCE_TOKENS, KEY_VALUE_HEADS * HEAD_SIZE).astype(jnp.bfloat16)
    return (grad_query, key_gradient_rows, value_gradient_rows, grad_proj)
```

```python
import functools
import math

import jax
import jax.numpy as jnp
from jax import lax
from jax.experimental import pallas as pl
from jax.experimental.pallas import tpu as pltpu
from jax.sharding import PartitionSpec as P

WIN = 4096
LOG2E = 1.4426950408889634
MESH = pl.DeviceIdType.MESH
NZ = 4
NEAR = (((1,), (1,)), ((), ()))


def gather_kernel(
    chunks,
    rows_hbm, ids_ref, gates_ref, resid_hbm, proj_hbm, attn_ref, key_hbm, value_hbm,
    gout_ref, gproj_ref, kx_hbm, vx_hbm,
    recv, hid, proj, attn_t, resid, pick, acc,
    a2a_send, a2a_recv, ag_send, ag_recv, kv_send, kv_recv, loc,
):
    seq = lax.axis_index("seq")
    me = lax.axis_index("head")
    n_seq = lax.axis_size("seq")
    z, x = me // 2, lax.rem(me, 2)
    heads = 2 * NZ
    tok, width = resid.shape
    cap = recv.shape[0] // heads
    w = width // chunks
    piece = w // 4
    span = kx_hbm.shape[0] // key_hbm.shape[0] - 1
    seq_dev = key_hbm.shape[0]

    def at(dz, flip):
        return lax.rem(z + dz, NZ) * 2 + (lax.rem(x + 1, 2) if flip else x)

    barrier = pltpu.get_barrier_semaphore()
    for d in range(1, heads):
        pl.semaphore_signal(barrier, inc=1, device_id=(seq, lax.rem(me + d, heads)), device_id_type=MESH)
    for d in range(1, span + 1):
        @pl.when(seq >= d)
        def _():
            pl.semaphore_signal(barrier, inc=1, device_id=(seq - d, me), device_id_type=MESH)
    pl.semaphore_wait(barrier, heads - 1 + jnp.minimum(span, n_seq - 1 - seq))

    def a2a(c, d):
        peer = lax.rem(me + d, heads)
        return pltpu.make_async_remote_copy(
            src_ref=rows_hbm.at[pl.ds(pl.multiple_of(peer * cap, cap), cap), pl.ds(c * w, w)],
            dst_ref=recv.at[pl.ds(pl.multiple_of(me * cap, cap), cap), pl.ds(c * w, w)],
            send_sem=a2a_send.at[c, d - 1],
            recv_sem=a2a_recv.at[c, d - 1],
            device_id=(seq, peer),
            device_id_type=MESH,
        )

    own = pl.ds(pl.multiple_of(me * cap, cap), cap)
    local = [
        pltpu.make_async_copy(rows_hbm.at[own, :], recv.at[own, :], loc.at[0]),
        pltpu.make_async_copy(resid_hbm, resid, loc.at[1]),
        pltpu.make_async_copy(proj_hbm, proj, loc.at[2]),
        pltpu.make_async_copy(key_hbm, kx_hbm.at[pl.ds(span * seq_dev, seq_dev), :], loc.at[3]),
        pltpu.make_async_copy(value_hbm, vx_hbm.at[pl.ds(span * seq_dev, seq_dev), :], loc.at[4]),
    ]
    for c in range(chunks):
        for d in (4, 5, 3, 2, 6, 1, 7):
            a2a(c, d).start()
        if c == 0:
            for copy in local:
                copy.start()

    def kv(d, which):
        src, dst = ((key_hbm, kx_hbm), (value_hbm, vx_hbm))[which]
        return pltpu.make_async_remote_copy(
            src_ref=src,
            dst_ref=dst.at[pl.ds((span - d) * seq_dev, seq_dev), :],
            send_sem=kv_send.at[d - 1, which],
            recv_sem=kv_recv.at[d - 1, which],
            device_id=(seq + d, me),
            device_id_type=MESH,
        )

    for d in range(1, span + 1):
        @pl.when(seq + d < n_seq)
        def _():
            kv(d, 0).start()
            kv(d, 1).start()

    ids = ids_ref[...]
    lane = lax.broadcasted_iota(jnp.int32, (tok, heads * cap), 1)
    expert, rank = lane // cap, lax.rem(lane, cap)
    hits = [(ids[:, k : k + 1] == expert) for k in range(2)]
    both = (hits[0] | hits[1]).astype(jnp.float32).astype(jnp.bfloat16)
    before = (lax.broadcasted_iota(jnp.int32, (tok, tok), 1) < lax.broadcasted_iota(jnp.int32, (tok, tok), 0))
    count = jnp.dot(before.astype(jnp.float32).astype(jnp.bfloat16), both, preferred_element_type=jnp.float32)
    here = count == rank.astype(jnp.float32)
    for k in range(2):
        pick[k] = (hits[k] & here).astype(jnp.float32).astype(jnp.bfloat16)
    for h in range(attn_ref.shape[0]):
        attn_t[h * 128 : (h + 1) * 128, :] = attn_ref[h].T
    acc[...] = jnp.zeros_like(acc)
    gates = gates_ref[...]
    for copy in local:
        copy.wait()

    def send(c, p, o, dz, flip, slot):
        block = hid.at[pl.ds(pl.multiple_of(o * tok, tok), tok), pl.ds(c * w + p * piece, piece)]
        return pltpu.make_async_remote_copy(
            src_ref=block,
            dst_ref=block,
            send_sem=ag_send.at[c, p, slot],
            recv_sem=ag_recv.at[c, p, o],
            device_id=(seq, at(dz, flip)),
            device_id_type=MESH,
        )

    def arrived(c, p, o):
        block = hid.at[pl.ds(pl.multiple_of(o * tok, tok), tok), pl.ds(c * w + p * piece, piece)]
        pltpu.make_async_remote_copy(
            src_ref=block, dst_ref=block, send_sem=ag_send.at[c, p, 0], recv_sem=ag_recv.at[c, p, o],
            device_id=(seq, at(0, True)), device_id_type=MESH,
        ).wait_recv()

    def first(c):
        for p in range(4):
            send(c, p, me, 0, True, 0).start()
            send(c, p, me, 1, False, 1).start()
            send(c, p, me, 3, False, 2).start()

    def second(c):
        for p in range(4):
            back, on = (3, 1) if p % 2 == 0 else (1, 3)
            arrived(c, p, at(back, False))
            send(c, p, at(back, False), on, False, 3).start()
            if p < 2:
                arrived(c, p, at(0, True))
                send(c, p, at(0, True), 1, False, 4).start()
                send(c, p, at(0, True), 3, False, 5).start()
            else:
                send(c, p, at(back, False), 0, True, 4).start()
                arrived(c, p, at(on, False))
                send(c, p, at(on, False), 0, True, 5).start()

    def third(c):
        for p in range(4):
            back, on = (3, 1) if p % 2 == 0 else (1, 3)
            if p < 2:
                arrived(c, p, at(back, True))
                send(c, p, at(back, True), on, False, 6).start()
            else:
                arrived(c, p, at(2, False))
                send(c, p, at(2, False), 0, True, 6).start()

    def rest(c):
        for p in range(4):
            back, on = (3, 1) if p % 2 == 0 else (1, 3)
            if p < 2:
                arrived(c, p, at(on, False))
                arrived(c, p, at(2, False))
                arrived(c, p, at(on, True))
                arrived(c, p, at(2, True))
            else:
                arrived(c, p, at(0, True))
                for dz in (1, 2, 3):
                    arrived(c, p, at(dz, True))

    def combine(c):
        for d in range(1, heads):
            a2a(c, d).wait_recv()
        tile = 256

        def body(t, _):
            cols = pl.ds(pl.multiple_of(c * w + t * tile, tile), tile)
            got = recv[:, cols]
            total = resid[:, cols].astype(jnp.float32)
            for k in range(2):
                total = total + gates[:, k : k + 1] * jnp.dot(pick[k], got, preferred_element_type=jnp.float32)
            hid[pl.ds(pl.multiple_of(me * tok, tok), tok), cols] = total.astype(jnp.bfloat16)
            return 0

        lax.fori_loop(0, w // tile, body, 0)

    def multiply(c):
        def rows_body(r, _):
            rows = pl.ds(pl.multiple_of(r * 256, 256), 256)
            acc[rows, :] += lax.dot_general(
                hid[rows, c * w : (c + 1) * w], proj[:, c * w : (c + 1) * w], NEAR,
                preferred_element_type=jnp.float32,
            )
            return 0

        lax.fori_loop(0, heads * tok // 256, rows_body, 0)

        def cols_body(t, _):
            cols = pl.ds(pl.multiple_of(c * w + t * 256, 256), 256)
            gproj_ref[:, cols] = jnp.dot(attn_t[...], hid[:, cols], preferred_element_type=jnp.float32).astype(jnp.bfloat16)
            return 0

        lax.fori_loop(0, w // 256, cols_body, 0)

    for t in range(chunks + 3):
        if t < chunks:
            combine(t)
            first(t)
        if 0 <= t - 1 < chunks:
            second(t - 1)
        if 0 <= t - 2 < chunks:
            third(t - 2)
        if 0 <= t - 3 < chunks:
            rest(t - 3)
            multiply(t - 3)
    gout_ref[...] = acc[...].astype(jnp.bfloat16)

    for c in range(chunks):
        for d in range(1, heads):
            a2a(c, d).wait_send()
        for p in range(4):
            for slot in range(7):
                send(c, p, me, 0, True, slot).wait_send()
    for d in range(1, span + 1):
        @pl.when(seq + d < n_seq)
        def _():
            kv(d, 0).wait_send()
            kv(d, 1).wait_send()
        @pl.when(seq >= d)
        def _():
            kv(d, 0).wait_recv()
            kv(d, 1).wait_recv()


def gathered(rows, ids, gates, resid, proj, attn, keys, values, chunks=4):
    tok, width = resid.shape
    heads = lax.axis_size("head")
    n, seq_dev, dim = attn.shape
    span = (WIN + seq_dev - 1) // seq_dev
    bf = jnp.bfloat16
    anyspace = pl.BlockSpec(memory_space=pl.ANY)
    vmem = pl.BlockSpec(memory_space=pltpu.VMEM)
    return pl.pallas_call(
        functools.partial(gather_kernel, chunks),
        out_shape=[
            jax.ShapeDtypeStruct((seq_dev, n * dim), bf),
            jax.ShapeDtypeStruct((n * dim, width), bf),
            jax.ShapeDtypeStruct(((span + 1) * seq_dev, dim), bf),
            jax.ShapeDtypeStruct(((span + 1) * seq_dev, dim), bf),
        ],
        in_specs=[anyspace, vmem, vmem, anyspace, anyspace, vmem, anyspace, anyspace],
        out_specs=[vmem, vmem, anyspace, anyspace],
        scratch_shapes=[
            pltpu.VMEM(rows.shape, bf),
            pltpu.VMEM((heads * tok, width), bf),
            pltpu.VMEM(proj.shape, bf),
            pltpu.VMEM((n * dim, seq_dev), bf),
            pltpu.VMEM((tok, width), bf),
            pltpu.VMEM((2, tok, rows.shape[0]), bf),
            pltpu.VMEM((seq_dev, n * dim), jnp.float32),
            pltpu.SemaphoreType.DMA((chunks, heads - 1)),
            pltpu.SemaphoreType.DMA((chunks, heads - 1)),
            pltpu.SemaphoreType.DMA((chunks, 4, 7)),
            pltpu.SemaphoreType.DMA((chunks, 4, heads)),
            pltpu.SemaphoreType.DMA((span, 2)),
            pltpu.SemaphoreType.DMA((span, 2)),
            pltpu.SemaphoreType.DMA((5,)),
        ],
        compiler_params=pltpu.CompilerParams(
            collective_id=0, has_side_effects=True, vmem_limit_bytes=56 * 2**20
        ),
        cost_estimate=pl.CostEstimate(flops=10**10, bytes_accessed=50 * 2**20, transcendentals=0),
        name="combine_gather_project",
    )(rows, ids, gates, resid, proj, attn, keys, values)


def window_kernel(block, first_ref, q_ref, do_ref, k_ref, v_ref, kt_ref, lse_ref, delta_ref, dq_ref, dk_ref, dv_ref, dq_acc):
    groups = q_ref.shape[0]
    i = pl.program_id(0)
    scale = 1.0 / math.sqrt(128)

    @pl.when(i == 0)
    def _():
        dk_ref[...] = jnp.zeros_like(dk_ref)
        dv_ref[...] = jnp.zeros_like(dv_ref)

    dq_acc[...] = jnp.zeros_like(dq_acc)
    last = i + WIN // block

    def step(kb, mask):
        rows = pl.ds(pl.multiple_of(kb * block, block), block)
        k = k_ref[rows, :]
        v = v_ref[rows, :]
        dv = jnp.zeros((block, 128), jnp.float32)
        dk = jnp.zeros((block, 128), jnp.float32)
        for h in range(groups):
            q = q_ref[h]
            do = do_ref[:, h * 128 : (h + 1) * 128]
            s = lax.dot_general(k, q, NEAR, preferred_element_type=jnp.float32)
            dp = lax.dot_general(v, do, NEAR, preferred_element_type=jnp.float32)
            p = jnp.exp2(s * (LOG2E * scale) - lse_ref[h : h + 1, :])
            if mask is not None:
                p = jnp.where(mask, p, 0.0)
            ds = p * (dp - delta_ref[h : h + 1, :])
            pb = p.astype(jnp.bfloat16)
            db = ds.astype(jnp.bfloat16)
            dv = dv + jnp.dot(pb, do, preferred_element_type=jnp.float32)
            dk = dk + jnp.dot(db, q, preferred_element_type=jnp.float32)
            dq_acc[h] += jnp.dot(kt_ref[:, rows], db, preferred_element_type=jnp.float32)
        dv_ref[rows, :] += dv
        dk_ref[rows, :] += dk * scale

    key = lax.broadcasted_iota(jnp.int32, (block, block), 0)
    query = lax.broadcasted_iota(jnp.int32, (block, block), 1)
    start = first_ref[0]

    @pl.when(start <= i)
    def _():
        step(i, key > query)

    def loop(kb, _):
        step(kb, None)
        return 0

    lax.fori_loop(jnp.maximum(i + 1, start), last, loop, 0)
    step(last, key <= query)
    for h in range(groups):
        dq_ref[:, h * 128 : (h + 1) * 128] = (dq_acc[h].T * scale).astype(jnp.bfloat16)


def window_backward(first_key, q, do, kx, vx, lse, delta, block=512):
    groups, tokens, dim = q.shape
    keys = kx.shape[0]

    def full(shape):
        return pl.BlockSpec(shape, lambda i, *_: (0,) * len(shape))

    return pl.pallas_call(
        functools.partial(window_kernel, block),
        grid_spec=pltpu.PrefetchScalarGridSpec(
            num_scalar_prefetch=1,
            grid=(tokens // block,),
            in_specs=[
                pl.BlockSpec((groups, block, dim), lambda i, *_: (0, i, 0)),
                pl.BlockSpec((block, groups * dim), lambda i, *_: (i, 0)),
                full(kx.shape),
                full(vx.shape),
                full((dim, keys)),
                pl.BlockSpec((groups, block), lambda i, *_: (0, i)),
                pl.BlockSpec((groups, block), lambda i, *_: (0, i)),
            ],
            out_specs=[
                pl.BlockSpec((block, groups * dim), lambda i, *_: (i, 0)),
                full((keys, dim)),
                full((keys, dim)),
            ],
            scratch_shapes=[pltpu.VMEM((groups, dim, block), jnp.float32)],
        ),
        out_shape=[
            jax.ShapeDtypeStruct((tokens, groups * dim), jnp.bfloat16),
            jax.ShapeDtypeStruct((keys, dim), jnp.float32),
            jax.ShapeDtypeStruct((keys, dim), jnp.float32),
        ],
        compiler_params=pltpu.CompilerParams(vmem_limit_bytes=40 * 2**20),
        cost_estimate=pl.CostEstimate(
            flops=10 * groups * tokens * WIN * dim, bytes_accessed=10 * 2**20,
            transcendentals=groups * tokens * WIN,
        ),
        name="window_backward",
    )((first_key // block).reshape(1), q, do, kx, vx, kx.T, lse * LOG2E, delta)


def shifted(block, axis, distance):
    devices = range(lax.axis_size(axis))
    route = [(i - distance, i) for i in devices if i - distance in devices]
    return lax.ppermute(block, axis, route)


def local(
    out_grad, expert_rows, expert_ids, gates, out_proj, attention_output,
    saved_queries, saved_keys, saved_values, softmax_normalizer,
):
    heads_dev, seq_dev, head_dim = saved_queries.shape
    span = (WIN + seq_dev - 1) // seq_dev
    heads = lax.axis_size("head")
    grad_out, proj_part, kx, vx = gathered(
        expert_rows[0], expert_ids, gates, out_grad, out_proj, attention_output, saved_keys[0], saved_values[0]
    )
    part = lax.psum_scatter(proj_part, "seq", scatter_dimension=0, tiled=True)
    grad_proj = lax.all_gather(part, "seq", axis=0, tiled=True)
    head_grads = jnp.transpose(grad_out.reshape(seq_dev, heads_dev, head_dim), (1, 0, 2))
    delta = jnp.sum(head_grads.astype(jnp.float32) * attention_output.astype(jnp.float32), axis=2)
    seq_pos = lax.axis_index("seq").astype(jnp.int32)
    first_key = jnp.maximum(span - seq_pos, 0) * seq_dev
    dq, dk_ext, dv_ext = window_backward(first_key, saved_queries, grad_out, kx, vx, softmax_normalizer, delta)
    ext = jnp.concatenate([dk_ext, dv_ext], axis=1)
    total = ext[span * seq_dev :]
    for distance in range(1, span + 1):
        far = ext[(span - distance) * seq_dev : (span - distance + 1) * seq_dev].astype(jnp.bfloat16)
        total = total + shifted(far, "seq", -distance).astype(jnp.float32)
    mine = jnp.concatenate([dq, total.astype(jnp.bfloat16)], axis=1)
    tok = seq_dev // heads
    swapped = lax.all_to_all(mine.reshape(heads, tok, mine.shape[1]), "head", split_axis=0, concat_axis=0, tiled=True)
    rows = jnp.transpose(swapped, (1, 0, 2))
    width = heads_dev * head_dim
    return (
        rows[:, :, :width].reshape(tok, heads * width),
        rows[:, :, width : width + head_dim].reshape(tok, heads * head_dim),
        rows[:, :, width + head_dim :].reshape(tok, heads * head_dim),
        grad_proj,
    )


def solution(mesh):
    in_specs = (
        P(("seq", "head"), None),
        P("head", "seq", None),
        P(("seq", "head"), None),
        P(("seq", "head"), None),
        P("head", None),
        P("head", "seq", None),
        P("head", "seq", None),
        P("head", "seq", None),
        P("head", "seq", None),
        P("head", "seq"),
    )
    out_specs = (
        P(("seq", "head"), None),
        P(("seq", "head"), None),
        P(("seq", "head"), None),
        P("head", None),
    )
    return jax.shard_map(local, mesh=mesh, in_specs=in_specs, out_specs=out_specs, check_vma=False)
```

```python
import functools
import math

import jax
import jax.numpy as jnp
from jax import lax
from jax.experimental import pallas as pl
from jax.experimental.pallas import tpu as pltpu
from jax.sharding import PartitionSpec as P

WIN = 4096
LOG2E = 1.4426950408889634
MESH = pl.DeviceIdType.MESH
NEAR = (((1,), (1,)), ((), ()))
BF = jnp.bfloat16
F32 = jnp.float32

NZ, NY = 4, 4
HEADS = 8
CHUNKS = 4
HALVES = 2
SPAN = 4
BLK = 512
UNITS = ((0, 0), (1, 0), (0, 1), (1, 1), (0, 2), (0, 3), (1, 2), (1, 3))


def layer_kernel(
    rows_hbm, ids_ref, gates_ref, resid_hbm, proj_hbm, attn_hbm, q_hbm, key_hbm, value_hbm, lse_ref,
    dq_hbm, dk_hbm, dv_hbm, gproj_hbm,
    recv, hid, proj, attn, attn_t, resid, pick, acc, gout, delta, qv, kx, vx, kt, dk, dv, dq_acc, dqs,
    r1, r2, s2, t3, r3, gfin, kvs, rc, rm1, rm2, kvf,
    a2a_send, a2a_recv, ag_send, ag_recv, kv_send, kv_recv,
    gp_send, gp_recv, dq_send, dq_recv, dkv_send, dkv_recv, fin_send, fin_recv, loc, loc_q, loc_out,
):
    seq = lax.axis_index("seq")
    me = lax.axis_index("head")
    n_seq = lax.axis_size("seq")
    z, x = me // 2, lax.rem(me, 2)
    core = lax.rem(seq, 2)
    y = lax.rem(seq // 2, NY)
    xlo = seq // (2 * NY)
    tok, width = resid.shape
    sub = tok // HALVES
    half = HEADS * sub
    cap = recv.shape[0] // HEADS
    w = width // CHUNKS
    cuts = (0, w // 3, 2 * w // 3, 5 * w // 6, w)
    wh = w // 2
    n_heads = attn.shape[1]
    dim = 128
    feats = n_heads * dim
    seq_dev = key_hbm.shape[0]
    scale = 1.0 / math.sqrt(dim)

    def mult(v, n):
        return pl.multiple_of(v, n)

    def at(dz, flip):
        return lax.rem(z + dz, NZ) * 2 + (lax.rem(x + 1, 2) if flip else x)

    sibling = seq + 1 - 2 * core
    across = lax.rem(seq + 2 * NY, 4 * NY)

    def along_y(d):
        return xlo * 2 * NY + lax.rem(y + d, NY) * 2 + core

    barrier = pltpu.get_barrier_semaphore()

    def greet(s, h):
        pl.semaphore_signal(barrier, inc=1, device_id=(s, h), device_id_type=MESH)

    for d in range(1, HEADS):
        greet(seq, lax.rem(me + d, HEADS))
    for d in range(1, 8):
        greet(lax.rem(seq + 2 * d, n_seq), me)
    greet(sibling, me)
    pl.semaphore_wait(barrier, HEADS - 1 + 8)

    def remote(src, dst, send, recv_sem, s, h):
        return pltpu.make_async_remote_copy(
            src_ref=src, dst_ref=dst, send_sem=send, recv_sem=recv_sem, device_id=(s, h), device_id_type=MESH
        )

    def a2a(c, d):
        peer = lax.rem(me + d, HEADS)
        return remote(
            rows_hbm.at[pl.ds(mult(peer * cap, cap), cap), pl.ds(c * w, w)],
            recv.at[pl.ds(mult(me * cap, cap), cap), pl.ds(c * w, w)],
            a2a_send.at[c, d - 1], a2a_recv.at[c, d - 1], seq, peer,
        )

    own = pl.ds(mult(me * cap, cap), cap)
    last_rows = pl.ds(SPAN * seq_dev, seq_dev)
    local = [
        pltpu.make_async_copy(rows_hbm.at[own, :], recv.at[own, :], loc.at[0]),
        pltpu.make_async_copy(resid_hbm, resid, loc.at[1]),
        pltpu.make_async_copy(proj_hbm, proj, loc.at[2]),
        pltpu.make_async_copy(key_hbm, kx.at[last_rows, :], loc.at[3]),
        pltpu.make_async_copy(value_hbm, vx.at[last_rows, :], loc.at[4]),
    ]
    for g in range(HALVES):
        for o in range(HEADS):
            there = pl.ds(o * tok + g * sub, sub)
            here = pl.ds(o * sub, sub)
            local.append(pltpu.make_async_copy(q_hbm.at[:, there, :], qv.at[g, :, here, :], loc_q.at[0, g, o]))
            local.append(pltpu.make_async_copy(attn_hbm.at[:, there, :], attn.at[g, :, here, :], loc_q.at[1, g, o]))
    def kv(k, which):
        arg, ext = ((key_hbm, kx), (value_hbm, vx))[which]
        sems = (kv_send.at[k, which], kv_recv.at[k, which])

        def slot(d):
            return ext.at[pl.ds(mult((SPAN - d) * seq_dev, seq_dev), seq_dev), :]

        if k == 0:
            return remote(arg, slot(2), *sems, seq + 2, me)
        if k == 1:
            return remote(arg, slot(4), *sems, seq + 4, me)
        if k == 2:
            return remote(slot(2 * core), slot(1), *sems, sibling, me)
        return remote(slot(2 + 2 * core), slot(3), *sems, sibling, me)

    def kv_start():
        @pl.when(seq + 4 < n_seq)
        def _():
            kv(1, 0).start()
            kv(1, 1).start()

        @pl.when(seq + 2 < n_seq)
        def _():
            kv(0, 0).start()
            kv(0, 1).start()

    def kv_pass():
        @pl.when(seq >= 2)
        def _():
            kv(0, 0).wait_recv()
            kv(0, 1).wait_recv()

        @pl.when(seq >= 4)
        def _():
            kv(1, 0).wait_recv()
            kv(1, 1).wait_recv()

        @pl.when((core == 0) | (seq >= 2))
        def _():
            kv(2, 0).start()
            kv(2, 1).start()

        @pl.when(seq >= 2 + 2 * core)
        def _():
            kv(3, 0).start()
            kv(3, 1).start()

    for c in range(CHUNKS):
        for d in (4, 5, 3, 2, 6, 1, 7):
            a2a(c, d).start()
        if c == 0:
            kv_start()
            for copy in local:
                copy.start()

    lane = lax.broadcasted_iota(jnp.int32, (tok, HEADS * cap), 1)
    expert, rank = (lane // cap).astype(F32), lax.rem(lane, cap).astype(F32)
    repeats = HEADS * cap // tok
    gates, hits = [], []
    for k in range(2):
        gates.append(jnp.broadcast_to(gates_ref[k : k + 1, :], (tok, tok)).T[:, 0:1])
        named = jnp.broadcast_to(ids_ref[k : k + 1, :].astype(F32), (tok, tok)).T
        hits.append(jnp.concatenate([named] * repeats, axis=1) == expert)
    both = (hits[0] | hits[1]).astype(F32).astype(BF)
    before = lax.broadcasted_iota(jnp.int32, (tok, tok), 1) < lax.broadcasted_iota(jnp.int32, (tok, tok), 0)
    count = jnp.dot(before.astype(F32).astype(BF), both, preferred_element_type=F32)
    here = count == rank
    for k in range(2):
        pick[k] = (hits[k] & here).astype(F32).astype(BF)
    acc[...] = jnp.zeros_like(acc)
    dk[...] = jnp.zeros_like(dk)
    dv[...] = jnp.zeros_like(dv)
    dq_acc[...] = jnp.zeros_like(dq_acc)
    for copy in local:
        copy.wait()
    for g in range(HALVES):
        for h in range(n_heads):
            attn_t[h * dim : (h + 1) * dim, g * half : (g + 1) * half] = attn[g, h].T

    def block(u, p, o):
        g, c = UNITS[u]
        return hid.at[pl.ds(mult(g * half + o * sub, sub), sub), pl.ds(c * w + cuts[p], cuts[p + 1] - cuts[p])]

    def send(u, p, o, dz, flip):
        return remote(block(u, p, o), block(u, p, o), ag_send.at[u], ag_recv.at[u, p, o], seq, at(dz, flip))

    def arrived(u, p, o):
        send(u, p, o, 0, True).wait_recv()

    def ways(p):
        return (3, 1) if p % 2 == 0 else (1, 3)

    def first(u):
        for p in range(4):
            send(u, p, me, 0, True).start()
            send(u, p, me, 1, False).start()
            send(u, p, me, 3, False).start()

    def second(u):
        for p in range(4):
            back, on = ways(p)
            arrived(u, p, at(back, False))
            send(u, p, at(back, False), on, False).start()
            if p < 2:
                arrived(u, p, at(0, True))
                send(u, p, at(0, True), 1, False).start()
                send(u, p, at(0, True), 3, False).start()
            else:
                send(u, p, at(back, False), 0, True).start()
                arrived(u, p, at(on, False))
                send(u, p, at(on, False), 0, True).start()

    def third(u):
        for p in range(4):
            back, on = ways(p)
            if p < 2:
                arrived(u, p, at(back, True))
                send(u, p, at(back, True), on, False).start()
            else:
                arrived(u, p, at(2, False))
                send(u, p, at(2, False), 0, True).start()

    def rest(u):
        for p in range(4):
            back, on = ways(p)
            if p < 2:
                arrived(u, p, at(on, False))
                arrived(u, p, at(2, False))
                arrived(u, p, at(on, True))
                arrived(u, p, at(2, True))
            else:
                for dz in range(NZ):
                    arrived(u, p, at(dz, True))

    def combine(c):
        for d in range(1, HEADS):
            a2a(c, d).wait_recv()
        tile = 256

        def body(t, _):
            cols = pl.ds(mult(c * w + t * tile, tile), tile)
            got = recv[:, cols]
            total = resid[:, cols].astype(F32)
            for k in range(2):
                total = total + gates[k] * jnp.dot(pick[k], got, preferred_element_type=F32)
            total = total.astype(BF)
            for g in range(HALVES):
                hid[pl.ds(mult(g * half + me * sub, sub), sub), cols] = total[g * sub : (g + 1) * sub]
            return 0

        lax.fori_loop(0, w // tile, body, 0)

    def project(u):
        g, c = UNITS[u]

        def body(r, _):
            rows = pl.ds(mult(r * 256, 256), 256)
            from_hid = pl.ds(mult(g * half + r * 256, 256), 256)
            acc[g, rows, :] += lax.dot_general(
                hid[from_hid, c * w : (c + 1) * w], proj[:, c * w : (c + 1) * w], NEAR, preferred_element_type=F32
            )
            return 0

        lax.fori_loop(0, half // 256, body, 0)

    def project_end(g):
        gout[g] = acc[g].astype(BF)
        for h in range(n_heads):
            turned = gout[g, :, h * dim : (h + 1) * dim].T.astype(F32)
            kept = attn_t[h * dim : (h + 1) * dim, g * half : (g + 1) * half].astype(F32)
            delta[g, h : h + 1, :] = jnp.sum(turned * kept, axis=0, keepdims=True)

    gpart = recv
    ry = feats // NY
    rx = ry // 2
    row_y = pl.ds(mult(y * ry, 16), ry)

    def mine(c, other=False):
        side = (1 - core) if other else core
        return pl.ds(mult(c * w + side * wh, 128), wh)

    def gp_copy(c, k):
        sems = (gp_send.at[c, k], gp_recv.at[c, k])
        if k == 0:
            return remote(gpart.at[pl.ds(0, feats), mine(c, True)], r1.at[c], *sems, sibling, me)
        if k <= 3:
            peer = pl.ds(mult(lax.rem(y + k, NY) * ry, 16), ry)
            return remote(gpart.at[peer, mine(c)], r2.at[c, k - 1], *sems, along_y(k), me)
        if k == 4:
            return remote(t3.at[c], r3.at[c], *sems, across, me)
        if k == 5:
            spot = gfin.at[pl.ds(mult(y * ry + xlo * rx, 16), rx), mine(c)]
            return remote(spot, spot, *sems, across, me)
        if k <= 8:
            return remote(gfin.at[row_y, mine(c)], gfin.at[row_y, mine(c)], *sems, along_y(k - 5), me)
        return remote(gfin.at[:, mine(c)], gfin.at[:, mine(c)], *sems, sibling, me)

    def gp0(c):
        def body(t, _):
            cols = pl.ds(mult(c * w + t * 256, 256), 256)
            gpart[pl.ds(0, feats), cols] = jnp.dot(attn_t[...], hid[:, cols], preferred_element_type=F32).astype(BF)
            return 0

        lax.fori_loop(0, w // 256, body, 0)
        gp_copy(c, 0).start()

    def gp1(c):
        gp_copy(c, 0).wait_recv()

        def body(r, _):
            rows = pl.ds(mult(r * 48, 16), 48)
            gpart[rows, mine(c)] = (gpart[rows, mine(c)].astype(F32) + r1[c, rows, :].astype(F32)).astype(BF)
            return 0

        lax.fori_loop(0, feats // 48, body, 0)
        for k in (1, 2, 3):
            gp_copy(c, k).start()

    def gp2(c):
        for k in (1, 2, 3):
            gp_copy(c, k).wait_recv()
        total = gpart[row_y, mine(c)].astype(F32)
        for k in range(3):
            total = total + r2[c, k].astype(F32)
        s2[c] = total
        t3[c] = s2[c, pl.ds(mult((1 - xlo) * rx, 16), rx), :].astype(BF)
        gp_copy(c, 4).start()

    def gp3(c):
        gp_copy(c, 4).wait_recv()
        total = s2[c, pl.ds(mult(xlo * rx, 16), rx), :] + r3[c].astype(F32)
        gfin[pl.ds(mult(y * ry + xlo * rx, 16), rx), mine(c)] = total.astype(BF)
        gp_copy(c, 5).start()

    def gp4(c):
        gp_copy(c, 5).wait_recv()
        for k in (6, 7, 8):
            gp_copy(c, k).start()

    def gp5(c):
        for k in (6, 7, 8):
            gp_copy(c, k).wait_recv()
        gp_copy(c, 9).start()

    def gp_out(c):
        return pltpu.make_async_copy(gfin.at[:, pl.ds(c * w, w)], gproj_hbm.at[:, pl.ds(c * w, w)], loc_out.at[c])

    def gp6(c):
        gp_copy(c, 9).wait_recv()
        gp_out(c).start()

    def attend(g, kb, lo, n, masked):
        rows = pl.ds(mult(kb * BLK, BLK), BLK)
        k = kx[rows, :]
        v = vx[rows, :]
        cols = slice(lo, lo + n)
        if masked:
            col = lax.broadcasted_iota(jnp.int32, (BLK, n), 1) + lo
            query = (col // sub) * tok + g * sub + lax.rem(col, sub)
            ago = query + WIN - (lax.broadcasted_iota(jnp.int32, (BLK, n), 0) + kb * BLK)
            keep = (ago >= 0) & (ago < WIN)
        ndv = jnp.zeros((BLK, dim), F32)
        ndk = jnp.zeros((BLK, dim), F32)
        for h in range(n_heads):
            q = qv[g, h, cols, :]
            do = gout[g, cols, h * dim : (h + 1) * dim]
            s = lax.dot_general(k, q, NEAR, preferred_element_type=F32)
            dp = lax.dot_general(v, do, NEAR, preferred_element_type=F32)
            p = jnp.exp2(s * (LOG2E * scale) - lse_ref[g, h : h + 1, cols])
            if masked:
                p = jnp.where(keep, p, 0.0)
            ds = p * (dp - delta[g, h : h + 1, cols])
            pb = p.astype(BF)
            db = ds.astype(BF)
            ndv = ndv + jnp.dot(pb, do, preferred_element_type=F32)
            ndk = ndk + jnp.dot(db, q, preferred_element_type=F32)
            dq_acc[h, :, cols] += jnp.dot(kt[:, rows], db, preferred_element_type=F32)
        dv[rows, :] += ndv
        dk[rows, :] += ndk * scale

    def dq_copy(g, d):
        o = lax.rem(me + d, HEADS)
        src = dqs.at[g, pl.ds(mult(o * sub, sub), sub), :]
        dst = dq_hbm.at[pl.ds(g * sub, sub), pl.ds(mult(me * feats, 128), feats)]
        if d == 0:
            return pltpu.make_async_copy(src, dst, loc_out.at[CHUNKS + g])
        return remote(src, dst, dq_send.at[g, d - 1], dq_recv.at[g, d - 1], seq, o)

    def dq_end(g):
        for h in range(n_heads):
            dqs[g, :, h * dim : (h + 1) * dim] = (dq_acc[h].T * scale).astype(BF)
        dq_acc[...] = jnp.zeros_like(dq_acc)
        for d in range(HEADS):
            dq_copy(g, d).start()

    def far(d):
        return pl.ds((SPAN - d) * seq_dev, seq_dev)

    def dkv_copy(k):
        sems = (dkv_send.at[k], dkv_recv.at[k])
        if k == 0:
            return remote(kvs.at[2], rc.at[0], *sems, sibling, me)
        if k == 1:
            return remote(kvs.at[0], rc.at[1], *sems, sibling, me)
        if k == 2:
            return remote(kvs.at[3], rm2, *sems, seq - 4, me)
        return remote(kvs.at[1], rm1, *sems, seq - 2, me)

    def pack(d, part=None):
        def body(r, _):
            rows = pl.ds(mult(r * 128, 128), 128)
            ext = pl.ds(mult((SPAN - d) * seq_dev + r * 128, 128), 128)
            for side, acc_ref in enumerate((dk, dv)):
                total = acc_ref[ext, :]
                if part is not None:
                    total = total + rc[part, rows, side * dim : (side + 1) * dim].astype(F32)
                kvs[d - 1, rows, side * dim : (side + 1) * dim] = total.astype(BF)
            return 0

        lax.fori_loop(0, seq_dev // 128, body, 0)

    def take(part):
        def body(r, _):
            rows = pl.ds(mult(r * 128, 128), 128)
            ext = pl.ds(mult(SPAN * seq_dev + r * 128, 128), 128)
            for side, acc_ref in enumerate((dk, dv)):
                acc_ref[ext, :] += part[rows, side * dim : (side + 1) * dim].astype(F32)
            return 0

        lax.fori_loop(0, seq_dev // 128, body, 0)

    def fin_copy(d, side):
        o = lax.rem(me + d, HEADS)
        src = kvf.at[side, pl.ds(mult(o * tok, tok), tok), :]
        dst = (dk_hbm, dv_hbm)[side].at[:, pl.ds(mult(me * dim, dim), dim)]
        if d == 0:
            return pltpu.make_async_copy(src, dst, loc_out.at[CHUNKS + HALVES + side])
        return remote(src, dst, fin_send.at[side, d - 1], fin_recv.at[side, d - 1], seq, o)

    def keys_ready():
        @pl.when((core == 1) | (seq >= 2))
        def _():
            kv(2, 0).wait_recv()
            kv(2, 1).wait_recv()

        @pl.when(seq >= 4 - 2 * core)
        def _():
            kv(3, 0).wait_recv()
            kv(3, 1).wait_recv()

        def body(r, _):
            rows = pl.ds(mult(r * BLK, BLK), BLK)
            @pl.when(r >= missing)
            def _():
                kt[:, rows] = kx[rows, :].T
            return 0

        lax.fori_loop(0, kx.shape[0] // BLK, body, 0)

    missing = jnp.maximum(SPAN - seq, 0) * (seq_dev // BLK)
    n_kb = kx.shape[0] // BLK

    def run(f, *a):
        return functools.partial(f, *a)

    units = len(UNITS)
    early = {
        4: [run(gp0, 0)],
        6: [run(gp1, 0), run(gp0, 1)],
        7: [run(gp2, 0), run(gp1, 1)],
        8: [run(gp3, 0), run(gp2, 1)],
    }
    for u in range(units + 1):
        if u < units:
            if UNITS[u][0] == 0:
                combine(UNITS[u][1])
            first(u)
        if u >= 1:
            second(u - 1)
        if u >= 2:
            third(u - 2)
        if u == 3:
            kv_pass()
        if u == 7:
            keys_ready()
        if u >= 3:
            rest(u - 3)
            project(u - 3)
        for action in early.get(u, ()):
            action()
    project_end(0)

    def after(step, actions):
        @pl.when(step)
        def _():
            for action in actions:
                action()

    plan = {
        1: [run(third, 7), run(gp4, 0), run(gp3, 1)],
        4: [run(rest, 6), run(project, 6), run(gp0, 2), run(gp5, 0), run(gp4, 1)],
        7: [run(gp1, 2), run(gp5, 1), run(gp6, 0)],
        8: [run(rest, 7), run(project, 7), run(gp0, 3)],
        9: [run(dq_end, 0), run(project_end, 1), run(gp2, 2), run(gp6, 1)],
        10: [run(gp1, 3)],
        11: [run(gp3, 2)],
        12: [run(gp2, 3), run(gp4, 2)],
        13: [run(pack, 3), dkv_copy(0).start],
        14: [run(gp3, 3), run(gp5, 2)],
        15: [dkv_copy(0).wait_recv, run(gp4, 3)],
        17: [run(pack, 1), dkv_copy(1).start, run(gp5, 3), run(gp6, 2)],
        19: [dkv_copy(1).wait_recv],
    }

    def step(j, _):
        g = j // n_kb
        kb = lax.rem(j, n_kb)

        def variant(which, lo, n, masked):
            @pl.when((kb >= missing) & which)
            def _():
                attend(g, kb, lo, n, masked)

        variant(kb == 0, 0, half // 2, True)
        variant((kb == 1) | (kb == n_kb - 2), 0, half, True)
        variant((kb > 1) & (kb < n_kb - 2), 0, half, False)
        variant(kb == n_kb - 1, half // 2, half // 2, True)
        for when in sorted(plan):
            after(j == when, plan[when])

        @pl.when((j == 15) & (core == 1))
        def _():
            pack(4, 0)

        @pl.when((j == 15) & (core == 0))
        def _():
            pack(4)

        @pl.when((j == 15) & (seq >= 4))
        def _():
            dkv_copy(2).start()

        @pl.when((j == 15) & (core == 0))
        def _():
            pack(2, 0)

        @pl.when((j == 15) & (core == 0) & (seq >= 2))
        def _():
            dkv_copy(3).start()

        @pl.when((j == 19) & (core == 1))
        def _():
            pack(2, 1)

        @pl.when((j == 19) & (core == 1) & (seq >= 2))
        def _():
            dkv_copy(3).start()

        return 0

    lax.fori_loop(0, HALVES * n_kb, step, 0)
    dq_end(1)
    gp6(3)

    @pl.when(core == 0)
    def _():
        take(rc.at[1])

    @pl.when(seq + 4 < n_seq)
    def _():
        dkv_copy(2).wait_recv()
        take(rm2)

    @pl.when(seq + 2 < n_seq)
    def _():
        dkv_copy(3).wait_recv()
        take(rm1)

    kvf[0] = dk[last_rows, :].astype(BF)
    kvf[1] = dv[last_rows, :].astype(BF)
    for d in range(HEADS):
        fin_copy(d, 0).start()
        fin_copy(d, 1).start()

    for c in range(CHUNKS):
        for d in range(1, HEADS):
            a2a(c, d).wait_send()
        for k in range(10):
            gp_copy(c, k).wait_send()
        gp_out(c).wait()
    for u in range(units):
        whole = hid.at[pl.ds(0, 7 * sub), pl.ds(0, w)]
        remote(whole, whole, ag_send.at[u], ag_recv.at[u, 0, 0], seq, at(0, True)).wait_send()
    for which in range(2):
        @pl.when(seq + 2 < n_seq)
        def _():
            kv(0, which).wait_send()

        @pl.when(seq + 4 < n_seq)
        def _():
            kv(1, which).wait_send()

        @pl.when((core == 0) | (seq >= 2))
        def _():
            kv(2, which).wait_send()

        @pl.when(seq >= 2 + 2 * core)
        def _():
            kv(3, which).wait_send()

    dkv_copy(0).wait_send()
    dkv_copy(1).wait_send()
    @pl.when(seq >= 4)
    def _():
        dkv_copy(2).wait_send()
    @pl.when(seq >= 2)
    def _():
        dkv_copy(3).wait_send()
    for g in range(HALVES):
        dq_copy(g, 0).wait()
        for d in range(1, HEADS):
            dq_copy(g, d).wait()
    for side in range(2):
        fin_copy(0, side).wait()
        for d in range(1, HEADS):
            fin_copy(d, side).wait()


def place_kernel(*refs):
    for source, target in zip(refs[:4], refs[4:]):
        target[...] = source[...]


def local(
    out_grad, expert_rows, expert_ids, gates, out_proj, attention_output,
    saved_queries, saved_keys, saved_values, softmax_normalizer,
):
    tok, width = out_grad.shape
    n, seq_dev, dim = saved_queries.shape
    feats = n * dim
    ext = (SPAN + 1) * seq_dev
    sub = tok // HALVES
    half = HEADS * sub
    units = HALVES * CHUNKS
    w = width // CHUNKS
    ry = feats // NY
    lse = (softmax_normalizer * LOG2E).reshape(n, HEADS, HALVES, sub)
    lse = jnp.transpose(lse, (2, 0, 1, 3)).reshape(HALVES, n, half)
    anyspace = pl.BlockSpec(memory_space=pl.ANY)
    vmem = pl.BlockSpec(memory_space=pltpu.VMEM)
    dma = pltpu.SemaphoreType.DMA
    results = pl.pallas_call(
        layer_kernel,
        out_shape=[
            jax.ShapeDtypeStruct((tok, HEADS * feats), BF),
            jax.ShapeDtypeStruct((tok, HEADS * dim), BF),
            jax.ShapeDtypeStruct((tok, HEADS * dim), BF),
            jax.ShapeDtypeStruct((feats, width), BF),
        ],
        in_specs=[anyspace, vmem, vmem] + [anyspace] * 6 + [vmem],
        out_specs=[anyspace] * 4,
        scratch_shapes=[
            pltpu.VMEM(expert_rows.shape[1:], BF),
            pltpu.VMEM((HEADS * tok, width), BF),
            pltpu.VMEM(out_proj.shape, BF),
            pltpu.VMEM((HALVES, n, half, dim), BF),
            pltpu.VMEM((feats, seq_dev), BF),
            pltpu.VMEM((tok, width), BF),
            pltpu.VMEM((2, tok, expert_rows.shape[1]), BF),
            pltpu.VMEM((HALVES, half, feats), F32),
            pltpu.VMEM((HALVES, half, feats), BF),
            pltpu.VMEM((HALVES, n, half), F32),
            pltpu.VMEM((HALVES, n, half, dim), BF),
            pltpu.VMEM((ext, dim), BF),
            pltpu.VMEM((ext, dim), BF),
            pltpu.VMEM((dim, ext), BF),
            pltpu.VMEM((ext, dim), F32),
            pltpu.VMEM((ext, dim), F32),
            pltpu.VMEM((n, dim, half), F32),
            pltpu.VMEM((HALVES, half, feats), BF),
            pltpu.VMEM((CHUNKS, feats, w // 2), BF),
            pltpu.VMEM((CHUNKS, 3, ry, w // 2), BF),
            pltpu.VMEM((CHUNKS, ry, w // 2), F32),
            pltpu.VMEM((CHUNKS, ry // 2, w // 2), BF),
            pltpu.VMEM((CHUNKS, ry // 2, w // 2), BF),
            pltpu.VMEM((feats, width), BF),
            pltpu.VMEM((SPAN, seq_dev, 2 * dim), BF),
            pltpu.VMEM((2, seq_dev, 2 * dim), BF),
            pltpu.VMEM((seq_dev, 2 * dim), BF),
            pltpu.VMEM((seq_dev, 2 * dim), BF),
            pltpu.VMEM((2, seq_dev, dim), BF),
            dma((CHUNKS, HEADS - 1)), dma((CHUNKS, HEADS - 1)),
            dma((units,)), dma((units, 4, HEADS)),
            dma((SPAN, 2)), dma((SPAN, 2)),
            dma((CHUNKS, 10)), dma((CHUNKS, 10)),
            dma((HALVES, HEADS - 1)), dma((HALVES, HEADS - 1)),
            dma((4,)), dma((4,)),
            dma((2, HEADS - 1)), dma((2, HEADS - 1)),
            dma((5,)), dma((2, HALVES, HEADS)), dma((CHUNKS + HALVES + 2,)),
        ],
        compiler_params=pltpu.CompilerParams(
            collective_id=0, has_side_effects=True, vmem_limit_bytes=62 * 2**20
        ),
        cost_estimate=pl.CostEstimate(flops=3 * 10**10, bytes_accessed=60 * 2**20, transcendentals=10**7),
        name="layer_backward",
    )(
        expert_rows[0], expert_ids.T, gates.T, out_grad, out_proj, attention_output,
        saved_queries, saved_keys[0], saved_values[0], lse,
    )
    steps = 8
    slabs = [pl.BlockSpec((r.shape[0] // steps, r.shape[1]), lambda i: (i, 0)) for r in results]
    return pl.pallas_call(
        place_kernel,
        grid=(steps,),
        out_shape=[jax.ShapeDtypeStruct(r.shape, r.dtype) for r in results],
        in_specs=slabs,
        out_specs=slabs,
        name="place_results",
    )(*results)


def solution(mesh):
    tokens = P(("seq", "head"), None)
    by_head = P("head", "seq", None)
    return jax.shard_map(
        local,
        mesh=mesh,
        in_specs=(tokens, by_head, tokens, tokens, P("head", None)) + (by_head,) * 4 + (P("head", "seq"),),
        out_specs=(tokens, tokens, tokens, P("head", None)),
        check_vma=False,
    )
```

```python
import functools
import math

import jax
import jax.numpy as jnp
from jax import lax
from jax.experimental import pallas as pl
from jax.experimental.pallas import tpu as pltpu
from jax.sharding import PartitionSpec as P

WIN = 4096
LOG2E = 1.4426950408889634
MESH = pl.DeviceIdType.MESH
NEAR = (((1,), (1,)), ((), ()))
BF = jnp.bfloat16
F32 = jnp.float32

NZ, NY = 4, 4
HEADS = 8
CHUNKS = 4
HALVES = 2
SPAN = 4
BLK = 512
UNITS = ((0, 0), (1, 0), (0, 1), (1, 1), (0, 2), (1, 2), (0, 3), (1, 3))


def layer_kernel(
    rows_hbm, ids_ref, gates_ref, resid_hbm, proj_hbm, attn_hbm, q_hbm, key_hbm, value_hbm, lse_ref,
    dq_hbm, dk_hbm, dv_hbm, gproj_hbm,
    recv, hid, proj, attn, attn_t, resid, pick, acc, gout, delta, qv, kx, vx, kt, dk, dv, dq_acc, dqs,
    r1, r2, s2, t3, r3, gfin, kvs, rc, rm1, rm2, kvf,
    a2a_send, a2a_recv, ag_send, ag_recv, kv_send, kv_recv,
    gp_send, gp_recv, dq_send, dq_recv, dkv_send, dkv_recv, fin_send, fin_recv, loc, loc_q, loc_out,
):
    seq = lax.axis_index("seq")
    me = lax.axis_index("head")
    n_seq = lax.axis_size("seq")
    z, x = me // 2, lax.rem(me, 2)
    core = lax.rem(seq, 2)
    y = lax.rem(seq // 2, NY)
    xlo = seq // (2 * NY)
    tok, width = resid.shape
    sub = tok // HALVES
    half = HEADS * sub
    cap = recv.shape[0] // HEADS
    w = width // CHUNKS
    wh = w // 2
    n_heads = attn.shape[1]
    dim = 128
    feats = n_heads * dim
    seq_dev = key_hbm.shape[0]
    scale = 1.0 / math.sqrt(dim)

    def mult(v, n):
        return pl.multiple_of(v, n)

    def at(dz, flip):
        return lax.rem(z + dz, NZ) * 2 + (lax.rem(x + 1, 2) if flip else x)

    sibling = seq + 1 - 2 * core
    across = lax.rem(seq + 2 * NY, 4 * NY)

    def along_y(d):
        return xlo * 2 * NY + lax.rem(y + d, NY) * 2 + core

    barrier = pltpu.get_barrier_semaphore()

    def greet(s, h):
        pl.semaphore_signal(barrier, inc=1, device_id=(s, h), device_id_type=MESH)

    for d in range(1, HEADS):
        greet(seq, lax.rem(me + d, HEADS))
    for d in range(1, 8):
        greet(lax.rem(seq + 2 * d, n_seq), me)
    greet(sibling, me)
    pl.semaphore_wait(barrier, HEADS - 1 + 8)

    def remote(src, dst, send, recv_sem, s, h):
        return pltpu.make_async_remote_copy(
            src_ref=src, dst_ref=dst, send_sem=send, recv_sem=recv_sem, device_id=(s, h), device_id_type=MESH
        )

    def a2a(c, d):
        peer = lax.rem(me + d, HEADS)
        return remote(
            rows_hbm.at[pl.ds(mult(peer * cap, cap), cap), pl.ds(c * w, w)],
            recv.at[pl.ds(mult(me * cap, cap), cap), pl.ds(c * w, w)],
            a2a_send.at[c, d - 1], a2a_recv.at[c, d - 1], seq, peer,
        )

    own = pl.ds(mult(me * cap, cap), cap)
    last_rows = pl.ds(SPAN * seq_dev, seq_dev)
    local = [
        pltpu.make_async_copy(rows_hbm.at[own, :], recv.at[own, :], loc.at[0]),
        pltpu.make_async_copy(resid_hbm, resid, loc.at[1]),
        pltpu.make_async_copy(proj_hbm, proj, loc.at[2]),
        pltpu.make_async_copy(key_hbm, kx.at[last_rows, :], loc.at[3]),
        pltpu.make_async_copy(value_hbm, vx.at[last_rows, :], loc.at[4]),
    ]
    for g in range(HALVES):
        for o in range(HEADS):
            there = pl.ds(o * tok + g * sub, sub)
            here = pl.ds(o * sub, sub)
            local.append(pltpu.make_async_copy(q_hbm.at[:, there, :], qv.at[g, :, here, :], loc_q.at[0, g, o]))
            local.append(pltpu.make_async_copy(attn_hbm.at[:, there, :], attn.at[g, :, here, :], loc_q.at[1, g, o]))
    def kv(k, which):
        arg, ext = ((key_hbm, kx), (value_hbm, vx))[which]
        sems = (kv_send.at[k, which], kv_recv.at[k, which])

        def slot(d):
            return ext.at[pl.ds(mult((SPAN - d) * seq_dev, seq_dev), seq_dev), :]

        if k == 0:
            return remote(arg, slot(2), *sems, seq + 2, me)
        if k == 1:
            return remote(arg, slot(4), *sems, seq + 4, me)
        if k == 2:
            return remote(slot(2 * core), slot(1), *sems, sibling, me)
        return remote(slot(2 + 2 * core), slot(3), *sems, sibling, me)

    def kv_start():
        @pl.when(seq + 4 < n_seq)
        def _():
            kv(1, 0).start()
            kv(1, 1).start()

        @pl.when(seq + 2 < n_seq)
        def _():
            kv(0, 0).start()
            kv(0, 1).start()

    def kv_pass():
        @pl.when(seq >= 2)
        def _():
            kv(0, 0).wait_recv()
            kv(0, 1).wait_recv()

        @pl.when(seq >= 4)
        def _():
            kv(1, 0).wait_recv()
            kv(1, 1).wait_recv()

        @pl.when((core == 0) | (seq >= 2))
        def _():
            kv(2, 0).start()
            kv(2, 1).start()

        @pl.when(seq >= 2 + 2 * core)
        def _():
            kv(3, 0).start()
            kv(3, 1).start()

    for c in range(CHUNKS):
        for d in (4, 5, 3, 2, 6, 1, 7):
            a2a(c, d).start()
        if c == 0:
            kv_start()
            for copy in local:
                copy.start()

    lane = lax.broadcasted_iota(jnp.int32, (tok, HEADS * cap), 1)
    expert, rank = (lane // cap).astype(F32), lax.rem(lane, cap).astype(F32)
    repeats = HEADS * cap // tok
    gates, hits = [], []
    for k in range(2):
        gates.append(jnp.broadcast_to(gates_ref[k : k + 1, :], (tok, tok)).T[:, 0:1])
        named = jnp.broadcast_to(ids_ref[k : k + 1, :].astype(F32), (tok, tok)).T
        hits.append(jnp.concatenate([named] * repeats, axis=1) == expert)
    both = (hits[0] | hits[1]).astype(F32).astype(BF)
    before = lax.broadcasted_iota(jnp.int32, (tok, tok), 1) < lax.broadcasted_iota(jnp.int32, (tok, tok), 0)
    count = jnp.dot(before.astype(F32).astype(BF), both, preferred_element_type=F32)
    here = count == rank
    for k in range(2):
        pick[k] = (hits[k] & here).astype(F32).astype(BF)
    acc[...] = jnp.zeros_like(acc)
    dk[...] = jnp.zeros_like(dk)
    dv[...] = jnp.zeros_like(dv)
    dq_acc[...] = jnp.zeros_like(dq_acc)
    for copy in local:
        copy.wait()
    for g in range(HALVES):
        for h in range(n_heads):
            attn_t[h * dim : (h + 1) * dim, g * half : (g + 1) * half] = attn[g, h].T

    cuts = (0, w // 6, w // 2, 5 * w // 6, w)
    everything, x_first, forward, backward = (0, 4), (1, 3), (0, 2), (2, 4)
    quarter = ((0, 1), (1, 2), (2, 3), (3, 4))

    def send(u, o, part, sem, dz, flip):
        g, c = UNITS[u]
        lo, hi = cuts[part[0]], cuts[part[1]]
        block = hid.at[pl.ds(mult(g * half + o * sub, sub), sub), pl.ds(c * w + lo, hi - lo)]
        return remote(block, block, ag_send.at[u], ag_recv.at[u, o, sem], seq, at(dz, flip))

    def arrived(u, o, part, sem):
        send(u, o, part, sem, 0, True).wait_recv()

    def first(u):
        send(u, me, everything, 0, 0, True).start()
        send(u, me, everything, 0, 1, False).start()
        send(u, me, everything, 0, 3, False).start()

    def second(u):
        arrived(u, at(3, False), everything, 0)
        send(u, at(3, False), forward, 0, 1, False).start()
        arrived(u, at(0, True), everything, 0)
        send(u, at(0, True), x_first, 0, 3, False).start()
        send(u, at(0, True), x_first, 0, 1, False).start()
        arrived(u, at(1, False), everything, 0)
        send(u, at(1, False), backward, 1, 3, False).start()
        for dz in (3, 1):
            send(u, at(dz, False), quarter[0], 1, 0, True).start()
            send(u, at(dz, False), quarter[3], 2, 0, True).start()

    def third(u):
        arrived(u, at(3, True), x_first, 0)
        send(u, at(3, True), quarter[1], 0, 1, False).start()
        arrived(u, at(1, True), x_first, 0)
        send(u, at(1, True), quarter[2], 3, 3, False).start()
        arrived(u, at(2, False), forward, 0)
        send(u, at(2, False), quarter[0], 1, 0, True).start()
        arrived(u, at(2, False), backward, 1)
        send(u, at(2, False), quarter[3], 2, 0, True).start()

    def rest(u):
        for dz in (1, 2, 3):
            arrived(u, at(dz, True), quarter[0], 1)
            arrived(u, at(dz, True), quarter[3], 2)
        arrived(u, at(2, True), quarter[1], 0)
        arrived(u, at(2, True), quarter[2], 3)

    def combine(c):
        for d in range(1, HEADS):
            a2a(c, d).wait_recv()
        tile = 256

        def body(t, _):
            cols = pl.ds(mult(c * w + t * tile, tile), tile)
            got = recv[:, cols]
            total = resid[:, cols].astype(F32)
            for k in range(2):
                total = total + gates[k] * jnp.dot(pick[k], got, preferred_element_type=F32)
            total = total.astype(BF)
            for g in range(HALVES):
                hid[pl.ds(mult(g * half + me * sub, sub), sub), cols] = total[g * sub : (g + 1) * sub]
            return 0

        lax.fori_loop(0, w // tile, body, 0)

    def project(u):
        g, c = UNITS[u]

        def body(r, _):
            rows = pl.ds(mult(r * 256, 256), 256)
            from_hid = pl.ds(mult(g * half + r * 256, 256), 256)
            acc[g, rows, :] += lax.dot_general(
                hid[from_hid, c * w : (c + 1) * w], proj[:, c * w : (c + 1) * w], NEAR, preferred_element_type=F32
            )
            return 0

        lax.fori_loop(0, half // 256, body, 0)

    def project_end(g):
        gout[g] = acc[g].astype(BF)
        for h in range(n_heads):
            turned = gout[g, :, h * dim : (h + 1) * dim].T.astype(F32)
            kept = attn_t[h * dim : (h + 1) * dim, g * half : (g + 1) * half].astype(F32)
            delta[g, h : h + 1, :] = jnp.sum(turned * kept, axis=0, keepdims=True)

    gpart = recv
    ry = feats // NY
    rx = ry // 2
    row_y = pl.ds(mult(y * ry, 16), ry)

    def mine(c, other=False):
        side = (1 - core) if other else core
        return pl.ds(mult(c * w + side * wh, 128), wh)

    def gp_copy(c, k):
        sems = (gp_send.at[c, k], gp_recv.at[c, k])
        if k == 0:
            return remote(gpart.at[pl.ds(0, feats), mine(c, True)], r1.at[c], *sems, sibling, me)
        if k <= 3:
            peer = pl.ds(mult(lax.rem(y + k, NY) * ry, 16), ry)
            return remote(gpart.at[peer, mine(c)], r2.at[c, k - 1], *sems, along_y(k), me)
        if k == 4:
            return remote(t3.at[c], r3.at[c], *sems, across, me)
        if k == 5:
            spot = gfin.at[pl.ds(mult(y * ry + xlo * rx, 16), rx), mine(c)]
            return remote(spot, spot, *sems, across, me)
        if k <= 8:
            return remote(gfin.at[row_y, mine(c)], gfin.at[row_y, mine(c)], *sems, along_y(k - 5), me)
        return remote(gfin.at[:, mine(c)], gfin.at[:, mine(c)], *sems, sibling, me)

    def gp0(c):
        def body(t, _):
            cols = pl.ds(mult(c * w + t * 256, 256), 256)
            gpart[pl.ds(0, feats), cols] = jnp.dot(attn_t[...], hid[:, cols], preferred_element_type=F32).astype(BF)
            return 0

        lax.fori_loop(0, w // 256, body, 0)
        gp_copy(c, 0).start()

    def gp1(c):
        gp_copy(c, 0).wait_recv()

        def body(r, _):
            rows = pl.ds(mult(r * 48, 16), 48)
            gpart[rows, mine(c)] = (gpart[rows, mine(c)].astype(F32) + r1[c, rows, :].astype(F32)).astype(BF)
            return 0

        lax.fori_loop(0, feats // 48, body, 0)
        for k in (1, 2, 3):
            gp_copy(c, k).start()

    def gp2(c):
        for k in (1, 2, 3):
            gp_copy(c, k).wait_recv()
        total = gpart[row_y, mine(c)].astype(F32)
        for k in range(3):
            total = total + r2[c, k].astype(F32)
        s2[c] = total
        t3[c] = s2[c, pl.ds(mult((1 - xlo) * rx, 16), rx), :].astype(BF)
        gp_copy(c, 4).start()

    def gp3(c):
        gp_copy(c, 4).wait_recv()
        total = s2[c, pl.ds(mult(xlo * rx, 16), rx), :] + r3[c].astype(F32)
        gfin[pl.ds(mult(y * ry + xlo * rx, 16), rx), mine(c)] = total.astype(BF)
        gp_copy(c, 5).start()

    def gp4(c):
        gp_copy(c, 5).wait_recv()
        for k in (6, 7, 8):
            gp_copy(c, k).start()

    def gp5(c):
        for k in (6, 7, 8):
            gp_copy(c, k).wait_recv()
        gp_copy(c, 9).start()

    def gp_out(c):
        return pltpu.make_async_copy(gfin.at[:, pl.ds(c * w, w)], gproj_hbm.at[:, pl.ds(c * w, w)], loc_out.at[c])

    def gp6(c):
        gp_copy(c, 9).wait_recv()
        gp_out(c).start()

    def attend(g, kb, lo, n, masked):
        rows = pl.ds(mult(kb * BLK, BLK), BLK)
        k = kx[rows, :]
        v = vx[rows, :]
        cols = slice(lo, lo + n)
        if masked:
            col = lax.broadcasted_iota(jnp.int32, (BLK, n), 1) + lo
            query = (col // sub) * tok + g * sub + lax.rem(col, sub)
            ago = query + WIN - (lax.broadcasted_iota(jnp.int32, (BLK, n), 0) + kb * BLK)
            keep = (ago >= 0) & (ago < WIN)
        ndv = jnp.zeros((BLK, dim), F32)
        ndk = jnp.zeros((BLK, dim), F32)
        for h in range(n_heads):
            q = qv[g, h, cols, :]
            do = gout[g, cols, h * dim : (h + 1) * dim]
            s = lax.dot_general(k, q, NEAR, preferred_element_type=F32)
            dp = lax.dot_general(v, do, NEAR, preferred_element_type=F32)
            p = jnp.exp2(s * (LOG2E * scale) - lse_ref[g, h : h + 1, cols])
            if masked:
                p = jnp.where(keep, p, 0.0)
            ds = p * (dp - delta[g, h : h + 1, cols])
            pb = p.astype(BF)
            db = ds.astype(BF)
            ndv = ndv + jnp.dot(pb, do, preferred_element_type=F32)
            ndk = ndk + jnp.dot(db, q, preferred_element_type=F32)
            dq_acc[h, :, cols] += jnp.dot(kt[:, rows], db, preferred_element_type=F32)
        dv[rows, :] += ndv
        dk[rows, :] += ndk * scale

    def dq_copy(g, d):
        o = lax.rem(me + d, HEADS)
        src = dqs.at[g, pl.ds(mult(o * sub, sub), sub), :]
        dst = dq_hbm.at[pl.ds(g * sub, sub), pl.ds(mult(me * feats, 128), feats)]
        if d == 0:
            return pltpu.make_async_copy(src, dst, loc_out.at[CHUNKS + g])
        return remote(src, dst, dq_send.at[g, d - 1], dq_recv.at[g, d - 1], seq, o)

    def dq_end(g):
        for h in range(n_heads):
            dqs[g, :, h * dim : (h + 1) * dim] = (dq_acc[h].T * scale).astype(BF)
        dq_acc[...] = jnp.zeros_like(dq_acc)
        for d in range(HEADS):
            dq_copy(g, d).start()

    def far(d):
        return pl.ds((SPAN - d) * seq_dev, seq_dev)

    def dkv_copy(k):
        sems = (dkv_send.at[k], dkv_recv.at[k])
        if k == 0:
            return remote(kvs.at[2], rc.at[0], *sems, sibling, me)
        if k == 1:
            return remote(kvs.at[0], rc.at[1], *sems, sibling, me)
        if k == 2:
            return remote(kvs.at[3], rm2, *sems, seq - 4, me)
        return remote(kvs.at[1], rm1, *sems, seq - 2, me)

    def pack(d, part=None):
        def body(r, _):
            rows = pl.ds(mult(r * 128, 128), 128)
            ext = pl.ds(mult((SPAN - d) * seq_dev + r * 128, 128), 128)
            for side, acc_ref in enumerate((dk, dv)):
                total = acc_ref[ext, :]
                if part is not None:
                    total = total + rc[part, rows, side * dim : (side + 1) * dim].astype(F32)
                kvs[d - 1, rows, side * dim : (side + 1) * dim] = total.astype(BF)
            return 0

        lax.fori_loop(0, seq_dev // 128, body, 0)

    def take(part):
        def body(r, _):
            rows = pl.ds(mult(r * 128, 128), 128)
            ext = pl.ds(mult(SPAN * seq_dev + r * 128, 128), 128)
            for side, acc_ref in enumerate((dk, dv)):
                acc_ref[ext, :] += part[rows, side * dim : (side + 1) * dim].astype(F32)
            return 0

        lax.fori_loop(0, seq_dev // 128, body, 0)

    def fin_copy(d, side):
        o = lax.rem(me + d, HEADS)
        src = kvf.at[side, pl.ds(mult(o * tok, tok), tok), :]
        dst = (dk_hbm, dv_hbm)[side].at[:, pl.ds(mult(me * dim, dim), dim)]
        if d == 0:
            return pltpu.make_async_copy(src, dst, loc_out.at[CHUNKS + HALVES + side])
        return remote(src, dst, fin_send.at[side, d - 1], fin_recv.at[side, d - 1], seq, o)

    def keys_ready():
        @pl.when((core == 1) | (seq >= 2))
        def _():
            kv(2, 0).wait_recv()
            kv(2, 1).wait_recv()

        @pl.when(seq >= 4 - 2 * core)
        def _():
            kv(3, 0).wait_recv()
            kv(3, 1).wait_recv()

        def body(r, _):
            rows = pl.ds(mult(r * BLK, BLK), BLK)
            @pl.when(r >= missing)
            def _():
                kt[:, rows] = kx[rows, :].T
            return 0

        lax.fori_loop(0, kx.shape[0] // BLK, body, 0)

    missing = jnp.maximum(SPAN - seq, 0) * (seq_dev // BLK)
    n_kb = kx.shape[0] // BLK

    def run(f, *a):
        return functools.partial(f, *a)

    units = len(UNITS)
    early = {
        4: [run(gp0, 0)],
        5: [run(gp1, 0)],
        6: [run(gp2, 0), run(gp0, 1)],
        7: [run(gp3, 0), run(gp1, 1)],
        8: [run(gp4, 0), run(gp2, 1), run(gp0, 2)],
        9: [run(gp5, 0), run(gp3, 1), run(gp1, 2)],
    }
    for u in range(units + 2):
        if u < units:
            if UNITS[u][0] == 0:
                combine(UNITS[u][1])
            first(u)
        if 1 <= u <= units:
            second(u - 1)
        if u >= 2:
            third(u - 2)
        if u == 3:
            kv_pass()
        if u == 7:
            keys_ready()
        if u >= 3:
            rest(u - 3)
            project(u - 3)
        for action in early.get(u, ()):
            action()
    project_end(0)

    def after(step, actions):
        @pl.when(step)
        def _():
            for action in actions:
                action()

    plan = {
        1: [run(gp6, 0), run(gp4, 1), run(gp2, 2)],
        3: [run(rest, 7), run(gp0, 3), run(project, 7)],
        4: [run(gp5, 1), run(gp3, 2)],
        5: [run(gp1, 3)],
        6: [run(gp6, 1), run(gp4, 2)],
        8: [run(gp2, 3)],
        9: [run(dq_end, 0), run(project_end, 1), run(gp5, 2)],
        10: [run(gp3, 3)],
        12: [run(gp6, 2), run(gp4, 3)],
        13: [run(pack, 3), dkv_copy(0).start],
        15: [run(pack, 1), dkv_copy(1).start, run(gp5, 3), dkv_copy(0).wait_recv],
        17: [dkv_copy(1).wait_recv],
        18: [run(gp6, 3)],
    }

    def step(j, _):
        g = j // n_kb
        turn = lax.rem(j, n_kb)
        kb = turn + jnp.where((turn == 4) | (turn == 5), 2, jnp.where((turn == 6) | (turn == 7), -2, 0))

        def variant(which, lo, n, masked):
            @pl.when((kb >= missing) & which)
            def _():
                attend(g, kb, lo, n, masked)

        variant(kb == 0, 0, half // 2, True)
        variant((kb == 1) | (kb == n_kb - 2), 0, half, True)
        variant((kb > 1) & (kb < n_kb - 2), 0, half, False)
        variant(kb == n_kb - 1, half // 2, half // 2, True)
        for when in sorted(plan):
            after(j == when, plan[when])

        @pl.when((j == 15) & (core == 1))
        def _():
            pack(4, 0)

        @pl.when((j == 15) & (core == 0))
        def _():
            pack(4)

        @pl.when((j == 15) & (seq >= 4))
        def _():
            dkv_copy(2).start()

        @pl.when((j == 17) & (core == 0))
        def _():
            pack(2, 0)

        @pl.when((j == 17) & (core == 1))
        def _():
            pack(2, 1)

        @pl.when((j == 17) & (seq >= 2))
        def _():
            dkv_copy(3).start()

        return 0

    lax.fori_loop(0, HALVES * n_kb, step, 0)
    dq_end(1)

    @pl.when(core == 0)
    def _():
        take(rc.at[1])

    @pl.when(seq + 4 < n_seq)
    def _():
        dkv_copy(2).wait_recv()
        take(rm2)

    @pl.when(seq + 2 < n_seq)
    def _():
        dkv_copy(3).wait_recv()
        take(rm1)

    kvf[0] = dk[last_rows, :].astype(BF)
    kvf[1] = dv[last_rows, :].astype(BF)
    for d in range(HEADS):
        fin_copy(d, 0).start()
        fin_copy(d, 1).start()

    for c in range(CHUNKS):
        for d in range(1, HEADS):
            a2a(c, d).wait_send()
        for k in range(10):
            gp_copy(c, k).wait_send()
        gp_out(c).wait()
    for u in range(units):
        whole = hid.at[pl.ds(0, 7 * sub), pl.ds(0, w)]
        remote(whole, whole, ag_send.at[u], ag_recv.at[u, 0, 0], seq, at(0, True)).wait_send()
    for which in range(2):
        @pl.when(seq + 2 < n_seq)
        def _():
            kv(0, which).wait_send()

        @pl.when(seq + 4 < n_seq)
        def _():
            kv(1, which).wait_send()

        @pl.when((core == 0) | (seq >= 2))
        def _():
            kv(2, which).wait_send()

        @pl.when(seq >= 2 + 2 * core)
        def _():
            kv(3, which).wait_send()

    dkv_copy(0).wait_send()
    dkv_copy(1).wait_send()
    @pl.when(seq >= 4)
    def _():
        dkv_copy(2).wait_send()
    @pl.when(seq >= 2)
    def _():
        dkv_copy(3).wait_send()
    for g in range(HALVES):
        dq_copy(g, 0).wait()
        for d in range(1, HEADS):
            dq_copy(g, d).wait()
    for side in range(2):
        fin_copy(0, side).wait()
        for d in range(1, HEADS):
            fin_copy(d, side).wait()


PLACES = tuple((3, i, 6) for i in range(6)) + tuple((0, i, 2) for i in range(2)) + ((1, 0, 1), (2, 0, 1))


def place_kernel(*refs):
    sources, targets, held, sems = refs[:4], refs[4:8], refs[8:12], refs[12]
    copies = []
    for i, (which, part, parts) in enumerate(PLACES):
        n = sources[which].shape[0] // parts
        rows = pl.ds(part * n, n)
        copies.append([
            pltpu.make_async_copy(sources[which].at[rows, :], held[which].at[rows, :], sems.at[0, i]),
            pltpu.make_async_copy(held[which].at[rows, :], targets[which].at[rows, :], sems.at[1, i]),
        ])
    for come, _ in copies:
        come.start()
    for come, go in copies:
        come.wait()
        go.start()
    for _, go in copies:
        go.wait()


def local(
    out_grad, expert_rows, expert_ids, gates, out_proj, attention_output,
    saved_queries, saved_keys, saved_values, softmax_normalizer,
):
    tok, width = out_grad.shape
    n, seq_dev, dim = saved_queries.shape
    feats = n * dim
    ext = (SPAN + 1) * seq_dev
    sub = tok // HALVES
    half = HEADS * sub
    units = HALVES * CHUNKS
    w = width // CHUNKS
    ry = feats // NY
    lse = (softmax_normalizer * LOG2E).reshape(n, HEADS, HALVES, sub)
    lse = jnp.transpose(lse, (2, 0, 1, 3)).reshape(HALVES, n, half)
    anyspace = pl.BlockSpec(memory_space=pl.ANY)
    vmem = pl.BlockSpec(memory_space=pltpu.VMEM)
    dma = pltpu.SemaphoreType.DMA
    results = pl.pallas_call(
        layer_kernel,
        out_shape=[
            jax.ShapeDtypeStruct((tok, HEADS * feats), BF),
            jax.ShapeDtypeStruct((tok, HEADS * dim), BF),
            jax.ShapeDtypeStruct((tok, HEADS * dim), BF),
            jax.ShapeDtypeStruct((feats, width), BF),
        ],
        in_specs=[anyspace, vmem, vmem] + [anyspace] * 6 + [vmem],
        out_specs=[anyspace] * 4,
        scratch_shapes=[
            pltpu.VMEM(expert_rows.shape[1:], BF),
            pltpu.VMEM((HEADS * tok, width), BF),
            pltpu.VMEM(out_proj.shape, BF),
            pltpu.VMEM((HALVES, n, half, dim), BF),
            pltpu.VMEM((feats, seq_dev), BF),
            pltpu.VMEM((tok, width), BF),
            pltpu.VMEM((2, tok, expert_rows.shape[1]), BF),
            pltpu.VMEM((HALVES, half, feats), F32),
            pltpu.VMEM((HALVES, half, feats), BF),
            pltpu.VMEM((HALVES, n, half), F32),
            pltpu.VMEM((HALVES, n, half, dim), BF),
            pltpu.VMEM((ext, dim), BF),
            pltpu.VMEM((ext, dim), BF),
            pltpu.VMEM((dim, ext), BF),
            pltpu.VMEM((ext, dim), F32),
            pltpu.VMEM((ext, dim), F32),
            pltpu.VMEM((n, dim, half), F32),
            pltpu.VMEM((HALVES, half, feats), BF),
            pltpu.VMEM((CHUNKS, feats, w // 2), BF),
            pltpu.VMEM((CHUNKS, 3, ry, w // 2), BF),
            pltpu.VMEM((CHUNKS, ry, w // 2), F32),
            pltpu.VMEM((CHUNKS, ry // 2, w // 2), BF),
            pltpu.VMEM((CHUNKS, ry // 2, w // 2), BF),
            pltpu.VMEM((feats, width), BF),
            pltpu.VMEM((SPAN, seq_dev, 2 * dim), BF),
            pltpu.VMEM((2, seq_dev, 2 * dim), BF),
            pltpu.VMEM((seq_dev, 2 * dim), BF),
            pltpu.VMEM((seq_dev, 2 * dim), BF),
            pltpu.VMEM((2, seq_dev, dim), BF),
            dma((CHUNKS, HEADS - 1)), dma((CHUNKS, HEADS - 1)),
            dma((units,)), dma((units, HEADS, 4)),
            dma((SPAN, 2)), dma((SPAN, 2)),
            dma((CHUNKS, 10)), dma((CHUNKS, 10)),
            dma((HALVES, HEADS - 1)), dma((HALVES, HEADS - 1)),
            dma((4,)), dma((4,)),
            dma((2, HEADS - 1)), dma((2, HEADS - 1)),
            dma((5,)), dma((2, HALVES, HEADS)), dma((CHUNKS + HALVES + 2,)),
        ],
        compiler_params=pltpu.CompilerParams(
            collective_id=0, has_side_effects=True, vmem_limit_bytes=62 * 2**20
        ),
        cost_estimate=pl.CostEstimate(flops=3 * 10**10, bytes_accessed=60 * 2**20, transcendentals=10**7),
        name="layer_backward",
    )(
        expert_rows[0], expert_ids.T, gates.T, out_grad, out_proj, attention_output,
        saved_queries, saved_keys[0], saved_values[0], lse,
    )
    return pl.pallas_call(
        place_kernel,
        out_shape=[jax.ShapeDtypeStruct(r.shape, r.dtype) for r in results],
        in_specs=[anyspace] * 4,
        out_specs=[anyspace] * 4,
        scratch_shapes=[pltpu.VMEM(r.shape, r.dtype) for r in results] + [dma((2, len(PLACES)))],
        compiler_params=pltpu.CompilerParams(vmem_limit_bytes=62 * 2**20),
        name="place_results",
    )(*results)


def solution(mesh):
    tokens = P(("seq", "head"), None)
    by_head = P("head", "seq", None)
    return jax.shard_map(
        local,
        mesh=mesh,
        in_specs=(tokens, by_head, tokens, tokens, P("head", None)) + (by_head,) * 4 + (P("head", "seq"),),
        out_specs=(tokens, tokens, tokens, P("head", None)),
        check_vma=False,
    )
```

```python
import functools
import math

import jax
import jax.numpy as jnp
from jax import lax
from jax.experimental import pallas as pl
from jax.experimental.pallas import tpu as pltpu
from jax.sharding import PartitionSpec as P

WIN = 4096
LOG2E = 1.4426950408889634
MESH = pl.DeviceIdType.MESH
NEAR = (((1,), (1,)), ((), ()))
BF = jnp.bfloat16
F32 = jnp.float32

NZ, NY = 4, 4
HEADS = 8
CHUNKS = 4
HALVES = 2
SPAN = 4
BLK = 512
UNITS = ((0, 0), (1, 0), (0, 1), (1, 1), (0, 2), (1, 2), (0, 3), (1, 3))


def layer_kernel(
    rows_hbm, ids_ref, gates_ref, resid_hbm, proj_hbm, attn_hbm, q_hbm, key_hbm, value_hbm, lse_ref,
    dq_hbm, dk_hbm, dv_hbm, gproj_hbm,
    recv, hid, proj, attn, attn_t, resid, pick, acc, gout, delta, qv, kx, vx, kt, dk, dv, dq_acc, dqs,
    r1, r2, s2, t3, r3, gfin, kvs, rc, rm1, rm2, kvf,
    a2a_send, a2a_recv, ag_send, ag_recv, kv_send, kv_recv,
    gp_send, gp_recv, dq_send, dq_recv, dkv_send, dkv_recv, fin_send, fin_recv, loc, loc_q, loc_out,
):
    seq = lax.axis_index("seq")
    me = lax.axis_index("head")
    n_seq = lax.axis_size("seq")
    z, x = me // 2, lax.rem(me, 2)
    core = lax.rem(seq, 2)
    y = lax.rem(seq // 2, NY)
    xlo = seq // (2 * NY)
    tok, width = resid.shape
    sub = tok // HALVES
    half = HEADS * sub
    cap = recv.shape[0] // HEADS
    w = width // CHUNKS
    wh = w // 2
    n_heads = attn.shape[1]
    dim = 128
    feats = n_heads * dim
    seq_dev = key_hbm.shape[0]
    scale = 1.0 / math.sqrt(dim)

    def mult(v, n):
        return pl.multiple_of(v, n)

    def at(dz, flip):
        return lax.rem(z + dz, NZ) * 2 + (lax.rem(x + 1, 2) if flip else x)

    sibling = seq + 1 - 2 * core
    across = lax.rem(seq + 2 * NY, 4 * NY)

    def along_y(d):
        return xlo * 2 * NY + lax.rem(y + d, NY) * 2 + core

    barrier = pltpu.get_barrier_semaphore()

    def greet(s, h):
        pl.semaphore_signal(barrier, inc=1, device_id=(s, h), device_id_type=MESH)

    for d in range(1, HEADS):
        greet(seq, lax.rem(me + d, HEADS))
    for d in range(1, 8):
        greet(lax.rem(seq + 2 * d, n_seq), me)
    greet(sibling, me)
    pl.semaphore_wait(barrier, HEADS - 1 + 8)

    def remote(src, dst, send, recv_sem, s, h):
        return pltpu.make_async_remote_copy(
            src_ref=src, dst_ref=dst, send_sem=send, recv_sem=recv_sem, device_id=(s, h), device_id_type=MESH
        )

    def a2a(c, d):
        peer = lax.rem(me + d, HEADS)
        return remote(
            rows_hbm.at[pl.ds(mult(peer * cap, cap), cap), pl.ds(c * w, w)],
            recv.at[pl.ds(mult(me * cap, cap), cap), pl.ds(c * w, w)],
            a2a_send.at[c, d - 1], a2a_recv.at[c, d - 1], seq, peer,
        )

    own = pl.ds(mult(me * cap, cap), cap)
    last_rows = pl.ds(SPAN * seq_dev, seq_dev)
    local = [
        pltpu.make_async_copy(rows_hbm.at[own, :], recv.at[own, :], loc.at[0]),
        pltpu.make_async_copy(resid_hbm, resid, loc.at[1]),
        pltpu.make_async_copy(proj_hbm, proj, loc.at[2]),
        pltpu.make_async_copy(key_hbm, kx.at[last_rows, :], loc.at[3]),
        pltpu.make_async_copy(value_hbm, vx.at[last_rows, :], loc.at[4]),
    ]
    for g in range(HALVES):
        for o in range(HEADS):
            there = pl.ds(o * tok + g * sub, sub)
            here = pl.ds(o * sub, sub)
            local.append(pltpu.make_async_copy(q_hbm.at[:, there, :], qv.at[g, :, here, :], loc_q.at[0, g, o]))
            local.append(pltpu.make_async_copy(attn_hbm.at[:, there, :], attn.at[g, :, here, :], loc_q.at[1, g, o]))
    def kv(k, which):
        arg, ext = ((key_hbm, kx), (value_hbm, vx))[which]
        sems = (kv_send.at[k, which], kv_recv.at[k, which])

        def slot(d):
            return ext.at[pl.ds(mult((SPAN - d) * seq_dev, seq_dev), seq_dev), :]

        if k == 0:
            return remote(arg, slot(2), *sems, seq + 2, me)
        if k == 1:
            return remote(arg, slot(4), *sems, seq + 4, me)
        if k == 2:
            return remote(slot(2 * core), slot(1), *sems, sibling, me)
        return remote(slot(2 + 2 * core), slot(3), *sems, sibling, me)

    def kv_start():
        @pl.when(seq + 4 < n_seq)
        def _():
            kv(1, 0).start()
            kv(1, 1).start()

        @pl.when(seq + 2 < n_seq)
        def _():
            kv(0, 0).start()
            kv(0, 1).start()

    def kv_pass():
        @pl.when(seq >= 2)
        def _():
            kv(0, 0).wait_recv()
            kv(0, 1).wait_recv()

        @pl.when(seq >= 4)
        def _():
            kv(1, 0).wait_recv()
            kv(1, 1).wait_recv()

        @pl.when((core == 0) | (seq >= 2))
        def _():
            kv(2, 0).start()
            kv(2, 1).start()

        @pl.when(seq >= 2 + 2 * core)
        def _():
            kv(3, 0).start()
            kv(3, 1).start()

    for c in range(CHUNKS):
        for d in (4, 5, 3, 2, 6, 1, 7):
            a2a(c, d).start()
        if c == 0:
            kv_start()
            for copy in local:
                copy.start()

    lane = lax.broadcasted_iota(jnp.int32, (tok, HEADS * cap), 1)
    expert, rank = (lane // cap).astype(F32), lax.rem(lane, cap).astype(F32)
    repeats = HEADS * cap // tok
    gates, hits = [], []
    for k in range(2):
        gates.append(jnp.broadcast_to(gates_ref[k : k + 1, :], (tok, tok)).T[:, 0:1])
        named = jnp.broadcast_to(ids_ref[k : k + 1, :].astype(F32), (tok, tok)).T
        hits.append(jnp.concatenate([named] * repeats, axis=1) == expert)
    both = (hits[0] | hits[1]).astype(F32).astype(BF)
    before = lax.broadcasted_iota(jnp.int32, (tok, tok), 1) < lax.broadcasted_iota(jnp.int32, (tok, tok), 0)
    count = jnp.dot(before.astype(F32).astype(BF), both, preferred_element_type=F32)
    here = count == rank
    for k in range(2):
        pick[k] = (hits[k] & here).astype(F32).astype(BF)
    acc[...] = jnp.zeros_like(acc)
    dk[...] = jnp.zeros_like(dk)
    dv[...] = jnp.zeros_like(dv)
    dq_acc[...] = jnp.zeros_like(dq_acc)
    for copy in local:
        copy.wait()
    for g in range(HALVES):
        for h in range(n_heads):
            attn_t[h * dim : (h + 1) * dim, g * half : (g + 1) * half] = attn[g, h].T

    cuts_of = ((0, w // 12, w // 2, 5 * w // 6, w), (0, w // 6, w // 2, 11 * w // 12, w))
    everything, x_first, forward, backward = (0, 4), (1, 3), (0, 2), (2, 4)
    quarter = ((0, 1), (1, 2), (2, 3), (3, 4))

    def send(u, o, part, sem, dz, flip):
        g, c = UNITS[u]
        cuts = cuts_of[u % 2]
        lo, hi = cuts[part[0]], cuts[part[1]]
        block = hid.at[pl.ds(mult(g * half + o * sub, sub), sub), pl.ds(c * w + lo, hi - lo)]
        return remote(block, block, ag_send.at[u], ag_recv.at[u, o, sem], seq, at(dz, flip))

    def arrived(u, o, part, sem):
        send(u, o, part, sem, 0, True).wait_recv()

    def first(u):
        send(u, me, everything, 0, 0, True).start()
        send(u, me, everything, 0, 1, False).start()
        send(u, me, everything, 0, 3, False).start()

    def second(u):
        arrived(u, at(3, False), everything, 0)
        send(u, at(3, False), forward, 0, 1, False).start()
        arrived(u, at(0, True), everything, 0)
        send(u, at(0, True), x_first, 0, 3, False).start()
        send(u, at(0, True), x_first, 0, 1, False).start()
        arrived(u, at(1, False), everything, 0)
        send(u, at(1, False), backward, 1, 3, False).start()
        for dz in (3, 1):
            send(u, at(dz, False), quarter[0], 1, 0, True).start()
            send(u, at(dz, False), quarter[3], 2, 0, True).start()

    def third(u):
        arrived(u, at(3, True), x_first, 0)
        send(u, at(3, True), quarter[1], 0, 1, False).start()
        arrived(u, at(1, True), x_first, 0)
        send(u, at(1, True), quarter[2], 3, 3, False).start()
        arrived(u, at(2, False), forward, 0)
        send(u, at(2, False), quarter[0], 1, 0, True).start()
        arrived(u, at(2, False), backward, 1)
        send(u, at(2, False), quarter[3], 2, 0, True).start()

    def rest(u):
        for dz in (1, 2, 3):
            arrived(u, at(dz, True), quarter[0], 1)
            arrived(u, at(dz, True), quarter[3], 2)
        arrived(u, at(2, True), quarter[1], 0)
        arrived(u, at(2, True), quarter[2], 3)

    def combine(c):
        for d in range(1, HEADS):
            a2a(c, d).wait_recv()
        tile = 256

        def body(t, _):
            cols = pl.ds(mult(c * w + t * tile, tile), tile)
            got = recv[:, cols]
            total = resid[:, cols].astype(F32)
            for k in range(2):
                total = total + gates[k] * jnp.dot(pick[k], got, preferred_element_type=F32)
            total = total.astype(BF)
            for g in range(HALVES):
                hid[pl.ds(mult(g * half + me * sub, sub), sub), cols] = total[g * sub : (g + 1) * sub]
            return 0

        lax.fori_loop(0, w // tile, body, 0)

    def project(u):
        g, c = UNITS[u]

        def body(r, _):
            rows = pl.ds(mult(r * 256, 256), 256)
            from_hid = pl.ds(mult(g * half + r * 256, 256), 256)
            acc[g, rows, :] += lax.dot_general(
                hid[from_hid, c * w : (c + 1) * w], proj[:, c * w : (c + 1) * w], NEAR, preferred_element_type=F32
            )
            return 0

        lax.fori_loop(0, half // 256, body, 0)

    def project_end(g):
        gout[g] = acc[g].astype(BF)
        for h in range(n_heads):
            turned = gout[g, :, h * dim : (h + 1) * dim].T.astype(F32)
            kept = attn_t[h * dim : (h + 1) * dim, g * half : (g + 1) * half].astype(F32)
            delta[g, h : h + 1, :] = jnp.sum(turned * kept, axis=0, keepdims=True)

    gpart = recv
    ry = feats // NY
    rx = ry // 2
    row_y = pl.ds(mult(y * ry, 16), ry)

    def mine(c, other=False):
        side = (1 - core) if other else core
        return pl.ds(mult(c * w + side * wh, 128), wh)

    def gp_copy(c, k):
        sems = (gp_send.at[c, k], gp_recv.at[c, k])
        if k == 0:
            return remote(gpart.at[pl.ds(0, feats), mine(c, True)], r1.at[c], *sems, sibling, me)
        if k <= 3:
            peer = pl.ds(mult(lax.rem(y + k, NY) * ry, 16), ry)
            return remote(gpart.at[peer, mine(c)], r2.at[c, k - 1], *sems, along_y(k), me)
        if k == 4:
            return remote(t3.at[c], r3.at[c], *sems, across, me)
        if k == 5:
            spot = gfin.at[pl.ds(mult(y * ry + xlo * rx, 16), rx), mine(c)]
            return remote(spot, spot, *sems, across, me)
        if k <= 8:
            return remote(gfin.at[row_y, mine(c)], gfin.at[row_y, mine(c)], *sems, along_y(k - 5), me)
        return remote(gfin.at[:, mine(c)], gfin.at[:, mine(c)], *sems, sibling, me)

    def gp0(c):
        def body(t, _):
            cols = pl.ds(mult(c * w + t * 256, 256), 256)
            gpart[pl.ds(0, feats), cols] = jnp.dot(attn_t[...], hid[:, cols], preferred_element_type=F32).astype(BF)
            return 0

        lax.fori_loop(0, w // 256, body, 0)
        gp_copy(c, 0).start()

    def gp1(c):
        gp_copy(c, 0).wait_recv()

        def body(r, _):
            rows = pl.ds(mult(r * 48, 16), 48)
            gpart[rows, mine(c)] = (gpart[rows, mine(c)].astype(F32) + r1[c, rows, :].astype(F32)).astype(BF)
            return 0

        lax.fori_loop(0, feats // 48, body, 0)
        for k in (1, 2, 3):
            gp_copy(c, k).start()

    def gp2(c):
        for k in (1, 2, 3):
            gp_copy(c, k).wait_recv()
        total = gpart[row_y, mine(c)].astype(F32)
        for k in range(3):
            total = total + r2[c, k].astype(F32)
        s2[c] = total
        t3[c] = s2[c, pl.ds(mult((1 - xlo) * rx, 16), rx), :].astype(BF)
        gp_copy(c, 4).start()

    def gp3(c):
        gp_copy(c, 4).wait_recv()
        total = s2[c, pl.ds(mult(xlo * rx, 16), rx), :] + r3[c].astype(F32)
        gfin[pl.ds(mult(y * ry + xlo * rx, 16), rx), mine(c)] = total.astype(BF)
        gp_copy(c, 5).start()

    def gp4(c):
        gp_copy(c, 5).wait_recv()
        for k in (6, 7, 8):
            gp_copy(c, k).start()

    def gp5(c):
        for k in (6, 7, 8):
            gp_copy(c, k).wait_recv()
        gp_copy(c, 9).start()

    def gp_out(c):
        return pltpu.make_async_copy(gfin.at[:, pl.ds(c * w, w)], gproj_hbm.at[:, pl.ds(c * w, w)], loc_out.at[c])

    def gp6(c):
        gp_copy(c, 9).wait_recv()
        gp_out(c).start()

    def attend(g, kb, lo, n, masked):
        rows = pl.ds(mult(kb * BLK, BLK), BLK)
        k = kx[rows, :]
        v = vx[rows, :]
        cols = slice(lo, lo + n)
        if masked:
            col = lax.broadcasted_iota(jnp.int32, (BLK, n), 1) + lo
            query = (col // sub) * tok + g * sub + lax.rem(col, sub)
            ago = query + WIN - (lax.broadcasted_iota(jnp.int32, (BLK, n), 0) + kb * BLK)
            keep = (ago >= 0) & (ago < WIN)
        ndv = jnp.zeros((BLK, dim), F32)
        ndk = jnp.zeros((BLK, dim), F32)
        for h in range(n_heads):
            q = qv[g, h, cols, :]
            do = gout[g, cols, h * dim : (h + 1) * dim]
            s = lax.dot_general(k, q, NEAR, preferred_element_type=F32)
            dp = lax.dot_general(v, do, NEAR, preferred_element_type=F32)
            p = jnp.exp2(s * (LOG2E * scale) - lse_ref[g, h : h + 1, cols])
            if masked:
                p = jnp.where(keep, p, 0.0)
            ds = p * (dp - delta[g, h : h + 1, cols])
            pb = p.astype(BF)
            db = ds.astype(BF)
            ndv = ndv + jnp.dot(pb, do, preferred_element_type=F32)
            ndk = ndk + jnp.dot(db, q, preferred_element_type=F32)
            dq_acc[h, :, cols] += jnp.dot(kt[:, rows], db, preferred_element_type=F32)
        dv[rows, :] += ndv
        dk[rows, :] += ndk * scale

    def dq_copy(g, d):
        o = lax.rem(me + d, HEADS)
        src = dqs.at[g, pl.ds(mult(o * sub, sub), sub), :]
        dst = dq_hbm.at[pl.ds(g * sub, sub), pl.ds(mult(me * feats, 128), feats)]
        if d == 0:
            return pltpu.make_async_copy(src, dst, loc_out.at[CHUNKS + g])
        return remote(src, dst, dq_send.at[g, d - 1], dq_recv.at[g, d - 1], seq, o)

    def dq_end(g):
        for h in range(n_heads):
            dqs[g, :, h * dim : (h + 1) * dim] = (dq_acc[h].T * scale).astype(BF)
        dq_acc[...] = jnp.zeros_like(dq_acc)
        for d in range(HEADS):
            dq_copy(g, d).start()

    def far(d):
        return pl.ds((SPAN - d) * seq_dev, seq_dev)

    def dkv_copy(k):
        sems = (dkv_send.at[k], dkv_recv.at[k])
        if k == 0:
            return remote(kvs.at[2], rc.at[0], *sems, sibling, me)
        if k == 1:
            return remote(kvs.at[0], rc.at[1], *sems, sibling, me)
        if k == 2:
            return remote(kvs.at[3], rm2, *sems, seq - 4, me)
        return remote(kvs.at[1], rm1, *sems, seq - 2, me)

    def pack(d, part=None):
        def body(r, _):
            rows = pl.ds(mult(r * 128, 128), 128)
            ext = pl.ds(mult((SPAN - d) * seq_dev + r * 128, 128), 128)
            for side, acc_ref in enumerate((dk, dv)):
                total = acc_ref[ext, :]
                if part is not None:
                    total = total + rc[part, rows, side * dim : (side + 1) * dim].astype(F32)
                kvs[d - 1, rows, side * dim : (side + 1) * dim] = total.astype(BF)
            return 0

        lax.fori_loop(0, seq_dev // 128, body, 0)

    def take(part):
        def body(r, _):
            rows = pl.ds(mult(r * 128, 128), 128)
            ext = pl.ds(mult(SPAN * seq_dev + r * 128, 128), 128)
            for side, acc_ref in enumerate((dk, dv)):
                acc_ref[ext, :] += part[rows, side * dim : (side + 1) * dim].astype(F32)
            return 0

        lax.fori_loop(0, seq_dev // 128, body, 0)

    def fin_copy(d, side):
        o = lax.rem(me + d, HEADS)
        src = kvf.at[side, pl.ds(mult(o * tok, tok), tok), :]
        dst = (dk_hbm, dv_hbm)[side].at[:, pl.ds(mult(me * dim, dim), dim)]
        if d == 0:
            return pltpu.make_async_copy(src, dst, loc_out.at[CHUNKS + HALVES + side])
        return remote(src, dst, fin_send.at[side, d - 1], fin_recv.at[side, d - 1], seq, o)

    def keys_ready():
        @pl.when((core == 1) | (seq >= 2))
        def _():
            kv(2, 0).wait_recv()
            kv(2, 1).wait_recv()

        @pl.when(seq >= 4 - 2 * core)
        def _():
            kv(3, 0).wait_recv()
            kv(3, 1).wait_recv()

        def body(r, _):
            rows = pl.ds(mult(r * BLK, BLK), BLK)
            @pl.when(r >= missing)
            def _():
                kt[:, rows] = kx[rows, :].T
            return 0

        lax.fori_loop(0, kx.shape[0] // BLK, body, 0)

    missing = jnp.maximum(SPAN - seq, 0) * (seq_dev // BLK)
    n_kb = kx.shape[0] // BLK

    def run(f, *a):
        return functools.partial(f, *a)

    units = len(UNITS)
    early = {
        4: [run(gp0, 0)],
        5: [run(gp1, 0)],
        6: [run(gp2, 0), run(gp0, 1)],
        7: [run(gp3, 0), run(gp1, 1)],
        8: [run(gp4, 0), run(gp2, 1), run(gp0, 2)],
        9: [run(gp5, 0), run(gp3, 1), run(gp1, 2)],
    }
    for u in range(units + 2):
        if u < units:
            if UNITS[u][0] == 0:
                combine(UNITS[u][1])
            first(u)
        if 1 <= u <= units:
            second(u - 1)
        if u >= 2:
            third(u - 2)
        if u == 3:
            kv_pass()
        if u == 7:
            keys_ready()
        if u >= 3:
            rest(u - 3)
            project(u - 3)
        for action in early.get(u, ()):
            action()
    project_end(0)

    def after(step, actions):
        @pl.when(step)
        def _():
            for action in actions:
                action()

    plan = {
        1: [run(gp6, 0), run(gp4, 1), run(gp2, 2)],
        3: [run(rest, 7), run(gp0, 3), run(project, 7)],
        4: [run(gp5, 1), run(gp3, 2)],
        5: [run(gp1, 3)],
        6: [run(gp6, 1), run(gp4, 2)],
        8: [run(gp2, 3)],
        9: [run(dq_end, 0), run(project_end, 1), run(gp5, 2)],
        10: [run(gp3, 3)],
        12: [run(gp6, 2), run(gp4, 3)],
        13: [run(pack, 3), dkv_copy(0).start],
        15: [run(pack, 1), dkv_copy(1).start, run(gp5, 3), dkv_copy(0).wait_recv],
        17: [dkv_copy(1).wait_recv],
        18: [run(gp6, 3)],
    }

    def step(j, _):
        g = j // n_kb
        turn = lax.rem(j, n_kb)
        kb = turn + jnp.where((turn == 4) | (turn == 5), 2, jnp.where((turn == 6) | (turn == 7), -2, 0))

        def variant(which, lo, n, masked):
            @pl.when((kb >= missing) & which)
            def _():
                attend(g, kb, lo, n, masked)

        variant(kb == 0, 0, half // 2, True)
        variant((kb == 1) | (kb == n_kb - 2), 0, half, True)
        variant((kb > 1) & (kb < n_kb - 2), 0, half, False)
        variant(kb == n_kb - 1, half // 2, half // 2, True)
        for when in sorted(plan):
            after(j == when, plan[when])

        @pl.when((j == 15) & (core == 1))
        def _():
            pack(4, 0)

        @pl.when((j == 15) & (core == 0))
        def _():
            pack(4)

        @pl.when((j == 15) & (seq >= 4))
        def _():
            dkv_copy(2).start()

        @pl.when((j == 17) & (core == 0))
        def _():
            pack(2, 0)

        @pl.when((j == 17) & (core == 1))
        def _():
            pack(2, 1)

        @pl.when((j == 17) & (seq >= 2))
        def _():
            dkv_copy(3).start()

        return 0

    lax.fori_loop(0, HALVES * n_kb, step, 0)
    dq_end(1)

    @pl.when(core == 0)
    def _():
        take(rc.at[1])

    @pl.when(seq + 4 < n_seq)
    def _():
        dkv_copy(2).wait_recv()
        take(rm2)

    @pl.when(seq + 2 < n_seq)
    def _():
        dkv_copy(3).wait_recv()
        take(rm1)

    kvf[0] = dk[last_rows, :].astype(BF)
    kvf[1] = dv[last_rows, :].astype(BF)
    for d in range(HEADS):
        fin_copy(d, 0).start()
        fin_copy(d, 1).start()

    for c in range(CHUNKS):
        for d in range(1, HEADS):
            a2a(c, d).wait_send()
        for k in range(10):
            gp_copy(c, k).wait_send()
        gp_out(c).wait()
    for u in range(units):
        whole = hid.at[pl.ds(0, 7 * sub), pl.ds(0, w)]
        remote(whole, whole, ag_send.at[u], ag_recv.at[u, 0, 0], seq, at(0, True)).wait_send()
    for which in range(2):
        @pl.when(seq + 2 < n_seq)
        def _():
            kv(0, which).wait_send()

        @pl.when(seq + 4 < n_seq)
        def _():
            kv(1, which).wait_send()

        @pl.when((core == 0) | (seq >= 2))
        def _():
            kv(2, which).wait_send()

        @pl.when(seq >= 2 + 2 * core)
        def _():
            kv(3, which).wait_send()

    dkv_copy(0).wait_send()
    dkv_copy(1).wait_send()
    @pl.when(seq >= 4)
    def _():
        dkv_copy(2).wait_send()
    @pl.when(seq >= 2)
    def _():
        dkv_copy(3).wait_send()
    for g in range(HALVES):
        dq_copy(g, 0).wait()
        for d in range(1, HEADS):
            dq_copy(g, d).wait()
    for side in range(2):
        fin_copy(0, side).wait()
        for d in range(1, HEADS):
            fin_copy(d, side).wait()


PLACES = tuple((3, i, 6) for i in range(6)) + tuple((0, i, 2) for i in range(2)) + ((1, 0, 1), (2, 0, 1))


def place_kernel(*refs):
    sources, targets, held, sems = refs[:4], refs[4:8], refs[8:12], refs[12]
    copies = []
    for i, (which, part, parts) in enumerate(PLACES):
        n = sources[which].shape[0] // parts
        rows = pl.ds(part * n, n)
        copies.append([
            pltpu.make_async_copy(sources[which].at[rows, :], held[which].at[rows, :], sems.at[0, i]),
            pltpu.make_async_copy(held[which].at[rows, :], targets[which].at[rows, :], sems.at[1, i]),
        ])
    for come, _ in copies:
        come.start()
    for come, go in copies:
        come.wait()
        go.start()
    for _, go in copies:
        go.wait()


def local(
    out_grad, expert_rows, expert_ids, gates, out_proj, attention_output,
    saved_queries, saved_keys, saved_values, softmax_normalizer,
):
    tok, width = out_grad.shape
    n, seq_dev, dim = saved_queries.shape
    feats = n * dim
    ext = (SPAN + 1) * seq_dev
    sub = tok // HALVES
    half = HEADS * sub
    units = HALVES * CHUNKS
    w = width // CHUNKS
    ry = feats // NY
    lse = (softmax_normalizer * LOG2E).reshape(n, HEADS, HALVES, sub)
    lse = jnp.transpose(lse, (2, 0, 1, 3)).reshape(HALVES, n, half)
    anyspace = pl.BlockSpec(memory_space=pl.ANY)
    vmem = pl.BlockSpec(memory_space=pltpu.VMEM)
    dma = pltpu.SemaphoreType.DMA
    results = pl.pallas_call(
        layer_kernel,
        out_shape=[
            jax.ShapeDtypeStruct((tok, HEADS * feats), BF),
            jax.ShapeDtypeStruct((tok, HEADS * dim), BF),
            jax.ShapeDtypeStruct((tok, HEADS * dim), BF),
            jax.ShapeDtypeStruct((feats, width), BF),
        ],
        in_specs=[anyspace, vmem, vmem] + [anyspace] * 6 + [vmem],
        out_specs=[anyspace] * 4,
        scratch_shapes=[
            pltpu.VMEM(expert_rows.shape[1:], BF),
            pltpu.VMEM((HEADS * tok, width), BF),
            pltpu.VMEM(out_proj.shape, BF),
            pltpu.VMEM((HALVES, n, half, dim), BF),
            pltpu.VMEM((feats, seq_dev), BF),
            pltpu.VMEM((tok, width), BF),
            pltpu.VMEM((2, tok, expert_rows.shape[1]), BF),
            pltpu.VMEM((HALVES, half, feats), F32),
            pltpu.VMEM((HALVES, half, feats), BF),
            pltpu.VMEM((HALVES, n, half), F32),
            pltpu.VMEM((HALVES, n, half, dim), BF),
            pltpu.VMEM((ext, dim), BF),
            pltpu.VMEM((ext, dim), BF),
            pltpu.VMEM((dim, ext), BF),
            pltpu.VMEM((ext, dim), F32),
            pltpu.VMEM((ext, dim), F32),
            pltpu.VMEM((n, dim, half), F32),
            pltpu.VMEM((HALVES, half, feats), BF),
            pltpu.VMEM((CHUNKS, feats, w // 2), BF),
            pltpu.VMEM((CHUNKS, 3, ry, w // 2), BF),
            pltpu.VMEM((CHUNKS, ry, w // 2), F32),
            pltpu.VMEM((CHUNKS, ry // 2, w // 2), BF),
            pltpu.VMEM((CHUNKS, ry // 2, w // 2), BF),
            pltpu.VMEM((feats, width), BF),
            pltpu.VMEM((SPAN, seq_dev, 2 * dim), BF),
            pltpu.VMEM((2, seq_dev, 2 * dim), BF),
            pltpu.VMEM((seq_dev, 2 * dim), BF),
            pltpu.VMEM((seq_dev, 2 * dim), BF),
            pltpu.VMEM((2, seq_dev, dim), BF),
            dma((CHUNKS, HEADS - 1)), dma((CHUNKS, HEADS - 1)),
            dma((units,)), dma((units, HEADS, 4)),
            dma((SPAN, 2)), dma((SPAN, 2)),
            dma((CHUNKS, 10)), dma((CHUNKS, 10)),
            dma((HALVES, HEADS - 1)), dma((HALVES, HEADS - 1)),
            dma((4,)), dma((4,)),
            dma((2, HEADS - 1)), dma((2, HEADS - 1)),
            dma((5,)), dma((2, HALVES, HEADS)), dma((CHUNKS + HALVES + 2,)),
        ],
        compiler_params=pltpu.CompilerParams(
            collective_id=0, has_side_effects=True, vmem_limit_bytes=62 * 2**20
        ),
        cost_estimate=pl.CostEstimate(flops=3 * 10**10, bytes_accessed=60 * 2**20, transcendentals=10**7),
        name="layer_backward",
    )(
        expert_rows[0], expert_ids.T, gates.T, out_grad, out_proj, attention_output,
        saved_queries, saved_keys[0], saved_values[0], lse,
    )
    return pl.pallas_call(
        place_kernel,
        out_shape=[jax.ShapeDtypeStruct(r.shape, r.dtype) for r in results],
        in_specs=[anyspace] * 4,
        out_specs=[anyspace] * 4,
        scratch_shapes=[pltpu.VMEM(r.shape, r.dtype) for r in results] + [dma((2, len(PLACES)))],
        compiler_params=pltpu.CompilerParams(vmem_limit_bytes=62 * 2**20),
        name="place_results",
    )(*results)


def solution(mesh):
    tokens = P(("seq", "head"), None)
    by_head = P("head", "seq", None)
    return jax.shard_map(
        local,
        mesh=mesh,
        in_specs=(tokens, by_head, tokens, tokens, P("head", None)) + (by_head,) * 4 + (P("head", "seq"),),
        out_specs=(tokens, tokens, tokens, P("head", None)),
        check_vma=False,
    )
```

```python
import functools
import math

import jax
import jax.numpy as jnp
from jax import lax
from jax.experimental import pallas as pl
from jax.experimental.pallas import tpu as pltpu
from jax.sharding import PartitionSpec as P

WIN = 4096
LOG2E = 1.4426950408889634
MESH = pl.DeviceIdType.MESH
NEAR = (((1,), (1,)), ((), ()))
BF = jnp.bfloat16
F32 = jnp.float32

NZ, NY = 4, 4
HEADS = 8
CHUNKS = 4
HALVES = 2
SPAN = 4
BLK = 512
UNITS = ((0, 0), (1, 0), (0, 1), (1, 1), (0, 2), (1, 2), (0, 3), (1, 3))


def layer_kernel(
    rows_hbm, ids_ref, gates_ref, resid_hbm, proj_hbm, attn_hbm, q_hbm, key_hbm, value_hbm, lse_ref,
    dq_hbm, dk_hbm, dv_hbm, gproj_hbm,
    recv, hid, proj, attn, attn_t, resid, pick, acc, gout, delta, qv, kx, vx, kt, dk, dv, dq_acc, dqs,
    r1, r2, s2, t3, r3, gfin, kvs, rc, rm1, rm2, kvf,
    a2a_send, a2a_recv, ag_send, ag_recv, kv_send, kv_recv,
    gp_send, gp_recv, dq_send, dq_recv, dkv_send, dkv_recv, fin_send, fin_recv, loc, loc_q, loc_out,
):
    seq = lax.axis_index("seq")
    me = lax.axis_index("head")
    n_seq = lax.axis_size("seq")
    z, x = me // 2, lax.rem(me, 2)
    core = lax.rem(seq, 2)
    y = lax.rem(seq // 2, NY)
    xlo = seq // (2 * NY)
    tok, width = resid.shape
    sub = tok // HALVES
    half = HEADS * sub
    cap = recv.shape[0] // HEADS
    w = width // CHUNKS
    wh = w // 2
    n_heads = attn.shape[1]
    dim = 128
    feats = n_heads * dim
    seq_dev = key_hbm.shape[0]
    scale = 1.0 / math.sqrt(dim)

    def mult(v, n):
        return pl.multiple_of(v, n)

    def at(dz, flip):
        return lax.rem(z + dz, NZ) * 2 + (lax.rem(x + 1, 2) if flip else x)

    sibling = seq + 1 - 2 * core
    across = lax.rem(seq + 2 * NY, 4 * NY)

    def along_y(d):
        return xlo * 2 * NY + lax.rem(y + d, NY) * 2 + core

    barrier = pltpu.get_barrier_semaphore()

    def greet(s, h):
        pl.semaphore_signal(barrier, inc=1, device_id=(s, h), device_id_type=MESH)

    for d in range(1, HEADS):
        greet(seq, lax.rem(me + d, HEADS))
    for d in range(1, 8):
        greet(lax.rem(seq + 2 * d, n_seq), me)
    greet(sibling, me)
    pl.semaphore_wait(barrier, HEADS - 1 + 8)

    def remote(src, dst, send, recv_sem, s, h):
        return pltpu.make_async_remote_copy(
            src_ref=src, dst_ref=dst, send_sem=send, recv_sem=recv_sem, device_id=(s, h), device_id_type=MESH
        )

    def a2a(c, d):
        peer = lax.rem(me + d, HEADS)
        return remote(
            rows_hbm.at[pl.ds(mult(peer * cap, cap), cap), pl.ds(c * w, w)],
            recv.at[pl.ds(mult(me * cap, cap), cap), pl.ds(c * w, w)],
            a2a_send.at[c, d - 1], a2a_recv.at[c, d - 1], seq, peer,
        )

    own = pl.ds(mult(me * cap, cap), cap)
    last_rows = pl.ds(SPAN * seq_dev, seq_dev)
    local = [
        pltpu.make_async_copy(rows_hbm.at[own, :], recv.at[own, :], loc.at[0]),
        pltpu.make_async_copy(resid_hbm, resid, loc.at[1]),
        pltpu.make_async_copy(proj_hbm, proj, loc.at[2]),
        pltpu.make_async_copy(key_hbm, kx.at[last_rows, :], loc.at[3]),
        pltpu.make_async_copy(value_hbm, vx.at[last_rows, :], loc.at[4]),
    ]
    for g in range(HALVES):
        for o in range(HEADS):
            there = pl.ds(o * tok + g * sub, sub)
            here = pl.ds(o * sub, sub)
            local.append(pltpu.make_async_copy(q_hbm.at[:, there, :], qv.at[g, :, here, :], loc_q.at[0, g, o]))
            local.append(pltpu.make_async_copy(attn_hbm.at[:, there, :], attn.at[g, :, here, :], loc_q.at[1, g, o]))
    def kv(k, which):
        arg, ext = ((key_hbm, kx), (value_hbm, vx))[which]
        sems = (kv_send.at[k, which], kv_recv.at[k, which])

        def slot(d):
            return ext.at[pl.ds(mult((SPAN - d) * seq_dev, seq_dev), seq_dev), :]

        if k == 0:
            return remote(arg, slot(2), *sems, seq + 2, me)
        if k == 1:
            return remote(arg, slot(4), *sems, seq + 4, me)
        if k == 2:
            return remote(slot(2 * core), slot(1), *sems, sibling, me)
        return remote(slot(2 + 2 * core), slot(3), *sems, sibling, me)

    def kv_start():
        @pl.when(seq + 4 < n_seq)
        def _():
            kv(1, 0).start()
            kv(1, 1).start()

        @pl.when(seq + 2 < n_seq)
        def _():
            kv(0, 0).start()
            kv(0, 1).start()

    def kv_pass():
        @pl.when(seq >= 2)
        def _():
            kv(0, 0).wait_recv()
            kv(0, 1).wait_recv()

        @pl.when(seq >= 4)
        def _():
            kv(1, 0).wait_recv()
            kv(1, 1).wait_recv()

        @pl.when((core == 0) | (seq >= 2))
        def _():
            kv(2, 0).start()
            kv(2, 1).start()

        @pl.when(seq >= 2 + 2 * core)
        def _():
            kv(3, 0).start()
            kv(3, 1).start()

    for c in range(CHUNKS):
        for d in (4, 5, 3, 2, 6, 1, 7):
            a2a(c, d).start()
        if c == 0:
            kv_start()
            for copy in local:
                copy.start()

    lane = lax.broadcasted_iota(jnp.int32, (tok, HEADS * cap), 1)
    expert, rank = (lane // cap).astype(F32), lax.rem(lane, cap).astype(F32)
    repeats = HEADS * cap // tok
    gates, hits = [], []
    for k in range(2):
        gates.append(jnp.broadcast_to(gates_ref[k : k + 1, :], (tok, tok)).T[:, 0:1])
        named = jnp.broadcast_to(ids_ref[k : k + 1, :].astype(F32), (tok, tok)).T
        hits.append(jnp.concatenate([named] * repeats, axis=1) == expert)
    both = (hits[0] | hits[1]).astype(F32).astype(BF)
    before = lax.broadcasted_iota(jnp.int32, (tok, tok), 1) < lax.broadcasted_iota(jnp.int32, (tok, tok), 0)
    count = jnp.dot(before.astype(F32).astype(BF), both, preferred_element_type=F32)
    here = count == rank
    for k in range(2):
        pick[k] = (hits[k] & here).astype(F32).astype(BF)
    acc[...] = jnp.zeros_like(acc)
    dk[...] = jnp.zeros_like(dk)
    dv[...] = jnp.zeros_like(dv)
    dq_acc[...] = jnp.zeros_like(dq_acc)
    for copy in local:
        copy.wait()
    for g in range(HALVES):
        for h in range(n_heads):
            attn_t[h * dim : (h + 1) * dim, g * half : (g + 1) * half] = attn[g, h].T

    cuts_of = ((0, w // 6, w // 2, 3 * w // 4, w), (0, w // 4, w // 2, 5 * w // 6, w))
    everything, x_first, forward, backward = (0, 4), (1, 3), (0, 2), (2, 4)
    quarter = ((0, 1), (1, 2), (2, 3), (3, 4))

    def send(u, o, part, sem, dz, flip):
        g, c = UNITS[u]
        cuts = cuts_of[u % 2]
        lo, hi = cuts[part[0]], cuts[part[1]]
        block = hid.at[pl.ds(mult(g * half + o * sub, sub), sub), pl.ds(c * w + lo, hi - lo)]
        return remote(block, block, ag_send.at[u], ag_recv.at[u, o, sem], seq, at(dz, flip))

    def arrived(u, o, part, sem):
        send(u, o, part, sem, 0, True).wait_recv()

    def first(u):
        send(u, me, everything, 0, 0, True).start()
        send(u, me, everything, 0, 1, False).start()
        send(u, me, everything, 0, 3, False).start()

    def second(u):
        arrived(u, at(3, False), everything, 0)
        send(u, at(3, False), forward, 0, 1, False).start()
        arrived(u, at(0, True), everything, 0)
        send(u, at(0, True), x_first, 0, 3, False).start()
        send(u, at(0, True), x_first, 0, 1, False).start()
        arrived(u, at(1, False), everything, 0)
        send(u, at(1, False), backward, 1, 3, False).start()
        for dz in (3, 1):
            send(u, at(dz, False), quarter[0], 1, 0, True).start()
            send(u, at(dz, False), quarter[3], 2, 0, True).start()

    def third(u):
        arrived(u, at(3, True), x_first, 0)
        send(u, at(3, True), quarter[1], 0, 1, False).start()
        arrived(u, at(1, True), x_first, 0)
        send(u, at(1, True), quarter[2], 3, 3, False).start()
        arrived(u, at(2, False), forward, 0)
        send(u, at(2, False), quarter[0], 1, 0, True).start()
        arrived(u, at(2, False), backward, 1)
        send(u, at(2, False), quarter[3], 2, 0, True).start()

    def rest(u):
        for dz in (1, 2, 3):
            arrived(u, at(dz, True), quarter[0], 1)
            arrived(u, at(dz, True), quarter[3], 2)
        arrived(u, at(2, True), quarter[1], 0)
        arrived(u, at(2, True), quarter[2], 3)

    def combine(c):
        for d in range(1, HEADS):
            a2a(c, d).wait_recv()
        tile = 256

        def body(t, _):
            cols = pl.ds(mult(c * w + t * tile, tile), tile)
            got = recv[:, cols]
            total = resid[:, cols].astype(F32)
            for k in range(2):
                total = total + gates[k] * jnp.dot(pick[k], got, preferred_element_type=F32)
            total = total.astype(BF)
            for g in range(HALVES):
                hid[pl.ds(mult(g * half + me * sub, sub), sub), cols] = total[g * sub : (g + 1) * sub]
            return 0

        lax.fori_loop(0, w // tile, body, 0)

    def project(u):
        g, c = UNITS[u]

        def body(r, _):
            rows = pl.ds(mult(r * 256, 256), 256)
            from_hid = pl.ds(mult(g * half + r * 256, 256), 256)
            acc[g, rows, :] += lax.dot_general(
                hid[from_hid, c * w : (c + 1) * w], proj[:, c * w : (c + 1) * w], NEAR, preferred_element_type=F32
            )
            return 0

        lax.fori_loop(0, half // 256, body, 0)

    def project_end(g):
        gout[g] = acc[g].astype(BF)
        for h in range(n_heads):
            turned = gout[g, :, h * dim : (h + 1) * dim].T.astype(F32)
            kept = attn_t[h * dim : (h + 1) * dim, g * half : (g + 1) * half].astype(F32)
            delta[g, h : h + 1, :] = jnp.sum(turned * kept, axis=0, keepdims=True)

    gpart = recv
    ry = feats // NY
    rx = ry // 2
    row_y = pl.ds(mult(y * ry, 16), ry)

    def mine(c, other=False):
        side = (1 - core) if other else core
        return pl.ds(mult(c * w + side * wh, 128), wh)

    def gp_copy(c, k):
        sems = (gp_send.at[c, k], gp_recv.at[c, k])
        if k == 0:
            return remote(gpart.at[pl.ds(0, feats), mine(c, True)], r1.at[c], *sems, sibling, me)
        if k <= 3:
            peer = pl.ds(mult(lax.rem(y + k, NY) * ry, 16), ry)
            return remote(gpart.at[peer, mine(c)], r2.at[c, k - 1], *sems, along_y(k), me)
        if k == 4:
            return remote(t3.at[c], r3.at[c], *sems, across, me)
        if k == 5:
            spot = gfin.at[pl.ds(mult(y * ry + xlo * rx, 16), rx), mine(c)]
            return remote(spot, spot, *sems, across, me)
        if k <= 8:
            return remote(gfin.at[row_y, mine(c)], gfin.at[row_y, mine(c)], *sems, along_y(k - 5), me)
        return remote(gfin.at[:, mine(c)], gfin.at[:, mine(c)], *sems, sibling, me)

    def gp0(c):
        def body(t, _):
            cols = pl.ds(mult(c * w + t * 256, 256), 256)
            gpart[pl.ds(0, feats), cols] = jnp.dot(attn_t[...], hid[:, cols], preferred_element_type=F32).astype(BF)
            return 0

        lax.fori_loop(0, w // 256, body, 0)
        gp_copy(c, 0).start()

    def gp1(c):
        gp_copy(c, 0).wait_recv()

        def body(r, _):
            rows = pl.ds(mult(r * 48, 16), 48)
            gpart[rows, mine(c)] = (gpart[rows, mine(c)].astype(F32) + r1[c, rows, :].astype(F32)).astype(BF)
            return 0

        lax.fori_loop(0, feats // 48, body, 0)
        for k in (1, 2, 3):
            gp_copy(c, k).start()

    def gp2(c):
        for k in (1, 2, 3):
            gp_copy(c, k).wait_recv()
        total = gpart[row_y, mine(c)].astype(F32)
        for k in range(3):
            total = total + r2[c, k].astype(F32)
        s2[c] = total
        t3[c] = s2[c, pl.ds(mult((1 - xlo) * rx, 16), rx), :].astype(BF)
        gp_copy(c, 4).start()

    def gp3(c):
        gp_copy(c, 4).wait_recv()
        total = s2[c, pl.ds(mult(xlo * rx, 16), rx), :] + r3[c].astype(F32)
        gfin[pl.ds(mult(y * ry + xlo * rx, 16), rx), mine(c)] = total.astype(BF)
        gp_copy(c, 5).start()

    def gp4(c):
        gp_copy(c, 5).wait_recv()
        for k in (6, 7, 8):
            gp_copy(c, k).start()

    def gp5(c):
        for k in (6, 7, 8):
            gp_copy(c, k).wait_recv()
        gp_copy(c, 9).start()

    def gp_out(c):
        return pltpu.make_async_copy(gfin.at[:, pl.ds(c * w, w)], gproj_hbm.at[:, pl.ds(c * w, w)], loc_out.at[c])

    def gp6(c):
        gp_copy(c, 9).wait_recv()
        gp_out(c).start()

    def attend(g, kb, lo, n, masked):
        rows = pl.ds(mult(kb * BLK, BLK), BLK)
        k = kx[rows, :]
        v = vx[rows, :]
        cols = slice(lo, lo + n)
        if masked:
            col = lax.broadcasted_iota(jnp.int32, (BLK, n), 1) + lo
            query = (col // sub) * tok + g * sub + lax.rem(col, sub)
            ago = query + WIN - (lax.broadcasted_iota(jnp.int32, (BLK, n), 0) + kb * BLK)
            keep = (ago >= 0) & (ago < WIN)
        ndv = jnp.zeros((BLK, dim), F32)
        ndk = jnp.zeros((BLK, dim), F32)
        for h in range(n_heads):
            q = qv[g, h, cols, :]
            do = gout[g, cols, h * dim : (h + 1) * dim]
            s = lax.dot_general(k, q, NEAR, preferred_element_type=F32)
            dp = lax.dot_general(v, do, NEAR, preferred_element_type=F32)
            p = jnp.exp2(s * (LOG2E * scale) - lse_ref[g, h : h + 1, cols])
            if masked:
                p = jnp.where(keep, p, 0.0)
            ds = p * (dp - delta[g, h : h + 1, cols])
            pb = p.astype(BF)
            db = ds.astype(BF)
            ndv = ndv + jnp.dot(pb, do, preferred_element_type=F32)
            ndk = ndk + jnp.dot(db, q, preferred_element_type=F32)
            dq_acc[h, :, cols] += jnp.dot(kt[:, rows], db, preferred_element_type=F32)
        dv[rows, :] += ndv
        dk[rows, :] += ndk * scale

    def dq_copy(g, d):
        o = lax.rem(me + d, HEADS)
        src = dqs.at[g, pl.ds(mult(o * sub, sub), sub), :]
        dst = dq_hbm.at[pl.ds(g * sub, sub), pl.ds(mult(me * feats, 128), feats)]
        if d == 0:
            return pltpu.make_async_copy(src, dst, loc_out.at[CHUNKS + g])
        return remote(src, dst, dq_send.at[g, d - 1], dq_recv.at[g, d - 1], seq, o)

    def dq_end(g):
        for h in range(n_heads):
            dqs[g, :, h * dim : (h + 1) * dim] = (dq_acc[h].T * scale).astype(BF)
        dq_acc[...] = jnp.zeros_like(dq_acc)
        for d in range(HEADS):
            dq_copy(g, d).start()

    def far(d):
        return pl.ds((SPAN - d) * seq_dev, seq_dev)

    def dkv_copy(k):
        sems = (dkv_send.at[k], dkv_recv.at[k])
        if k == 0:
            return remote(kvs.at[2], rc.at[0], *sems, sibling, me)
        if k == 1:
            return remote(kvs.at[0], rc.at[1], *sems, sibling, me)
        if k == 2:
            return remote(kvs.at[3], rm2, *sems, seq - 4, me)
        return remote(kvs.at[1], rm1, *sems, seq - 2, me)

    def pack(d, part=None):
        def body(r, _):
            rows = pl.ds(mult(r * 128, 128), 128)
            ext = pl.ds(mult((SPAN - d) * seq_dev + r * 128, 128), 128)
            for side, acc_ref in enumerate((dk, dv)):
                total = acc_ref[ext, :]
                if part is not None:
                    total = total + rc[part, rows, side * dim : (side + 1) * dim].astype(F32)
                kvs[d - 1, rows, side * dim : (side + 1) * dim] = total.astype(BF)
            return 0

        lax.fori_loop(0, seq_dev // 128, body, 0)

    def take(part):
        def body(r, _):
            rows = pl.ds(mult(r * 128, 128), 128)
            ext = pl.ds(mult(SPAN * seq_dev + r * 128, 128), 128)
            for side, acc_ref in enumerate((dk, dv)):
                acc_ref[ext, :] += part[rows, side * dim : (side + 1) * dim].astype(F32)
            return 0

        lax.fori_loop(0, seq_dev // 128, body, 0)

    def fin_copy(d, side):
        o = lax.rem(me + d, HEADS)
        src = kvf.at[side, pl.ds(mult(o * tok, tok), tok), :]
        dst = (dk_hbm, dv_hbm)[side].at[:, pl.ds(mult(me * dim, dim), dim)]
        if d == 0:
            return pltpu.make_async_copy(src, dst, loc_out.at[CHUNKS + HALVES + side])
        return remote(src, dst, fin_send.at[side, d - 1], fin_recv.at[side, d - 1], seq, o)

    def keys_ready():
        @pl.when((core == 1) | (seq >= 2))
        def _():
            kv(2, 0).wait_recv()
            kv(2, 1).wait_recv()

        @pl.when(seq >= 4 - 2 * core)
        def _():
            kv(3, 0).wait_recv()
            kv(3, 1).wait_recv()

        def body(r, _):
            rows = pl.ds(mult(r * BLK, BLK), BLK)
            @pl.when(r >= missing)
            def _():
                kt[:, rows] = kx[rows, :].T
            return 0

        lax.fori_loop(0, kx.shape[0] // BLK, body, 0)

    missing = jnp.maximum(SPAN - seq, 0) * (seq_dev // BLK)
    n_kb = kx.shape[0] // BLK

    def run(f, *a):
        return functools.partial(f, *a)

    units = len(UNITS)
    early = {
        4: [run(gp0, 0)],
        5: [run(gp1, 0)],
        6: [run(gp2, 0), run(gp0, 1)],
        7: [run(gp3, 0), run(gp1, 1)],
        8: [run(gp4, 0), run(gp2, 1), run(gp0, 2)],
        9: [run(gp5, 0), run(gp3, 1), run(gp1, 2)],
    }
    for u in range(units + 2):
        if u < units:
            if UNITS[u][0] == 0:
                combine(UNITS[u][1])
            first(u)
        if 1 <= u <= units:
            second(u - 1)
        if u >= 2:
            third(u - 2)
        if u == 3:
            kv_pass()
        if u == 7:
            keys_ready()
        if u >= 3:
            rest(u - 3)
            project(u - 3)
        for action in early.get(u, ()):
            action()
    project_end(0)

    def after(step, actions):
        @pl.when(step)
        def _():
            for action in actions:
                action()

    plan = {
        1: [run(gp6, 0), run(gp4, 1), run(gp2, 2)],
        3: [run(rest, 7), run(gp0, 3), run(project, 7)],
        4: [run(gp5, 1), run(gp3, 2)],
        5: [run(gp1, 3)],
        6: [run(gp6, 1), run(gp4, 2)],
        8: [run(gp2, 3)],
        9: [run(dq_end, 0), run(project_end, 1), run(gp5, 2)],
        10: [run(gp3, 3)],
        12: [run(gp6, 2), run(gp4, 3)],
        13: [run(pack, 3), dkv_copy(0).start],
        15: [run(pack, 1), dkv_copy(1).start, run(gp5, 3), dkv_copy(0).wait_recv],
        17: [dkv_copy(1).wait_recv],
        18: [run(gp6, 3)],
    }

    def step(j, _):
        g = j // n_kb
        turn = lax.rem(j, n_kb)
        kb = turn + jnp.where((turn == 4) | (turn == 5), 2, jnp.where((turn == 6) | (turn == 7), -2, 0))

        def variant(which, lo, n, masked):
            @pl.when((kb >= missing) & which)
            def _():
                attend(g, kb, lo, n, masked)

        variant(kb == 0, 0, half // 2, True)
        variant((kb == 1) | (kb == n_kb - 2), 0, half, True)
        variant((kb > 1) & (kb < n_kb - 2), 0, half, False)
        variant(kb == n_kb - 1, half // 2, half // 2, True)
        for when in sorted(plan):
            after(j == when, plan[when])

        @pl.when((j == 15) & (core == 1))
        def _():
            pack(4, 0)

        @pl.when((j == 15) & (core == 0))
        def _():
            pack(4)

        @pl.when((j == 15) & (seq >= 4))
        def _():
            dkv_copy(2).start()

        @pl.when((j == 17) & (core == 0))
        def _():
            pack(2, 0)

        @pl.when((j == 17) & (core == 1))
        def _():
            pack(2, 1)

        @pl.when((j == 17) & (seq >= 2))
        def _():
            dkv_copy(3).start()

        return 0

    lax.fori_loop(0, HALVES * n_kb, step, 0)
    dq_end(1)

    @pl.when(core == 0)
    def _():
        take(rc.at[1])

    @pl.when(seq + 4 < n_seq)
    def _():
        dkv_copy(2).wait_recv()
        take(rm2)

    @pl.when(seq + 2 < n_seq)
    def _():
        dkv_copy(3).wait_recv()
        take(rm1)

    kvf[0] = dk[last_rows, :].astype(BF)
    kvf[1] = dv[last_rows, :].astype(BF)
    for d in range(HEADS):
        fin_copy(d, 0).start()
        fin_copy(d, 1).start()

    for c in range(CHUNKS):
        for d in range(1, HEADS):
            a2a(c, d).wait_send()
        for k in range(10):
            gp_copy(c, k).wait_send()
        gp_out(c).wait()
    for u in range(units):
        whole = hid.at[pl.ds(0, 7 * sub), pl.ds(0, w)]
        remote(whole, whole, ag_send.at[u], ag_recv.at[u, 0, 0], seq, at(0, True)).wait_send()
    for which in range(2):
        @pl.when(seq + 2 < n_seq)
        def _():
            kv(0, which).wait_send()

        @pl.when(seq + 4 < n_seq)
        def _():
            kv(1, which).wait_send()

        @pl.when((core == 0) | (seq >= 2))
        def _():
            kv(2, which).wait_send()

        @pl.when(seq >= 2 + 2 * core)
        def _():
            kv(3, which).wait_send()

    dkv_copy(0).wait_send()
    dkv_copy(1).wait_send()
    @pl.when(seq >= 4)
    def _():
        dkv_copy(2).wait_send()
    @pl.when(seq >= 2)
    def _():
        dkv_copy(3).wait_send()
    for g in range(HALVES):
        dq_copy(g, 0).wait()
        for d in range(1, HEADS):
            dq_copy(g, d).wait()
    for side in range(2):
        fin_copy(0, side).wait()
        for d in range(1, HEADS):
            fin_copy(d, side).wait()


PLACES = tuple((3, i, 6) for i in range(6)) + tuple((0, i, 2) for i in range(2)) + ((1, 0, 1), (2, 0, 1))


def place_kernel(*refs):
    sources, targets, held, sems = refs[:4], refs[4:8], refs[8:12], refs[12]
    copies = []
    for i, (which, part, parts) in enumerate(PLACES):
        n = sources[which].shape[0] // parts
        rows = pl.ds(part * n, n)
        copies.append([
            pltpu.make_async_copy(sources[which].at[rows, :], held[which].at[rows, :], sems.at[0, i]),
            pltpu.make_async_copy(held[which].at[rows, :], targets[which].at[rows, :], sems.at[1, i]),
        ])
    for come, _ in copies:
        come.start()
    for come, go in copies:
        come.wait()
        go.start()
    for _, go in copies:
        go.wait()


def local(
    out_grad, expert_rows, expert_ids, gates, out_proj, attention_output,
    saved_queries, saved_keys, saved_values, softmax_normalizer,
):
    tok, width = out_grad.shape
    n, seq_dev, dim = saved_queries.shape
    feats = n * dim
    ext = (SPAN + 1) * seq_dev
    sub = tok // HALVES
    half = HEADS * sub
    units = HALVES * CHUNKS
    w = width // CHUNKS
    ry = feats // NY
    lse = (softmax_normalizer * LOG2E).reshape(n, HEADS, HALVES, sub)
    lse = jnp.transpose(lse, (2, 0, 1, 3)).reshape(HALVES, n, half)
    anyspace = pl.BlockSpec(memory_space=pl.ANY)
    vmem = pl.BlockSpec(memory_space=pltpu.VMEM)
    dma = pltpu.SemaphoreType.DMA
    results = pl.pallas_call(
        layer_kernel,
        out_shape=[
            jax.ShapeDtypeStruct((tok, HEADS * feats), BF),
            jax.ShapeDtypeStruct((tok, HEADS * dim), BF),
            jax.ShapeDtypeStruct((tok, HEADS * dim), BF),
            jax.ShapeDtypeStruct((feats, width), BF),
        ],
        in_specs=[anyspace, vmem, vmem] + [anyspace] * 6 + [vmem],
        out_specs=[anyspace] * 4,
        scratch_shapes=[
            pltpu.VMEM(expert_rows.shape[1:], BF),
            pltpu.VMEM((HEADS * tok, width), BF),
            pltpu.VMEM(out_proj.shape, BF),
            pltpu.VMEM((HALVES, n, half, dim), BF),
            pltpu.VMEM((feats, seq_dev), BF),
            pltpu.VMEM((tok, width), BF),
            pltpu.VMEM((2, tok, expert_rows.shape[1]), BF),
            pltpu.VMEM((HALVES, half, feats), F32),
            pltpu.VMEM((HALVES, half, feats), BF),
            pltpu.VMEM((HALVES, n, half), F32),
            pltpu.VMEM((HALVES, n, half, dim), BF),
            pltpu.VMEM((ext, dim), BF),
            pltpu.VMEM((ext, dim), BF),
            pltpu.VMEM((dim, ext), BF),
            pltpu.VMEM((ext, dim), F32),
            pltpu.VMEM((ext, dim), F32),
            pltpu.VMEM((n, dim, half), F32),
            pltpu.VMEM((HALVES, half, feats), BF),
            pltpu.VMEM((CHUNKS, feats, w // 2), BF),
            pltpu.VMEM((CHUNKS, 3, ry, w // 2), BF),
            pltpu.VMEM((CHUNKS, ry, w // 2), F32),
            pltpu.VMEM((CHUNKS, ry // 2, w // 2), BF),
            pltpu.VMEM((CHUNKS, ry // 2, w // 2), BF),
            pltpu.VMEM((feats, width), BF),
            pltpu.VMEM((SPAN, seq_dev, 2 * dim), BF),
            pltpu.VMEM((2, seq_dev, 2 * dim), BF),
            pltpu.VMEM((seq_dev, 2 * dim), BF),
            pltpu.VMEM((seq_dev, 2 * dim), BF),
            pltpu.VMEM((2, seq_dev, dim), BF),
            dma((CHUNKS, HEADS - 1)), dma((CHUNKS, HEADS - 1)),
            dma((units,)), dma((units, HEADS, 4)),
            dma((SPAN, 2)), dma((SPAN, 2)),
            dma((CHUNKS, 10)), dma((CHUNKS, 10)),
            dma((HALVES, HEADS - 1)), dma((HALVES, HEADS - 1)),
            dma((4,)), dma((4,)),
            dma((2, HEADS - 1)), dma((2, HEADS - 1)),
            dma((5,)), dma((2, HALVES, HEADS)), dma((CHUNKS + HALVES + 2,)),
        ],
        compiler_params=pltpu.CompilerParams(
            collective_id=0, has_side_effects=True, vmem_limit_bytes=62 * 2**20
        ),
        cost_estimate=pl.CostEstimate(flops=3 * 10**10, bytes_accessed=60 * 2**20, transcendentals=10**7),
        name="layer_backward",
    )(
        expert_rows[0], expert_ids.T, gates.T, out_grad, out_proj, attention_output,
        saved_queries, saved_keys[0], saved_values[0], lse,
    )
    return pl.pallas_call(
        place_kernel,
        out_shape=[jax.ShapeDtypeStruct(r.shape, r.dtype) for r in results],
        in_specs=[anyspace] * 4,
        out_specs=[anyspace] * 4,
        scratch_shapes=[pltpu.VMEM(r.shape, r.dtype) for r in results] + [dma((2, len(PLACES)))],
        compiler_params=pltpu.CompilerParams(vmem_limit_bytes=62 * 2**20),
        name="place_results",
    )(*results)


def solution(mesh):
    tokens = P(("seq", "head"), None)
    by_head = P("head", "seq", None)
    return jax.shard_map(
        local,
        mesh=mesh,
        in_specs=(tokens, by_head, tokens, tokens, P("head", None)) + (by_head,) * 4 + (P("head", "seq"),),
        out_specs=(tokens, tokens, tokens, P("head", None)),
        check_vma=False,
    )
```
